32 devices in a mesh: dp: 8 (over y, x, core), row: 4 (over z).
Axes of the slice: x: 2, y: 2, z: 4, core: 2. Of those that a mesh axis runs over, the one named last changes fastest.
Arguments:
- latent: bfloat16 [64, 12, 12, 256], P('dp', 'row'), may hold values from -6 to 6
- codes: int32 [64, 12, 12], P('dp', 'row'), may hold values from 0 to 16383
- codebook: bfloat16 [16384, 256], P('row'), may hold values from -6 to 6
- post_weight: bfloat16 [256, 256], replicated, may hold values from -0.375 to 0.375
- post_bias: float32 [256], replicated, may hold values from -3 to 3
- entry_weight: bfloat16 [9, 256, 512], replicated, may hold values from -0.125 to 0.125
- entry_bias: float32 [512], replicated, may hold values from -3 to 3
- first_gain: float32 [512], replicated, may hold values from 0.25 to 1.75
- first_shift: float32 [512], replicated, may hold values from -3 to 3
- first_weight: bfloat16 [9, 512, 512], replicated, may hold values from -0.09375 to 0.09375
- first_bias: float32 [512], replicated, may hold values from -3 to 3
- second_gain: float32 [512], replicated, may hold values from 0.25 to 1.75
- second_shift: float32 [512], replicated, may hold values from -3 to 3
- second_weight: bfloat16 [9, 512, 512], replicated, may hold values from -0.09375 to 0.09375
- second_bias: float32 [512], replicated, may hold values from -3 to 3
- mixer_gain: float32 [512], replicated, may hold values from 0.25 to 1.75
- mixer_shift: float32 [512], replicated, may hold values from -3 to 3
- query_weight: bfloat16 [512, 512], replicated, may hold values from -0.25 to 0.25
- query_bias: float32 [512], replicated, may hold values from -3 to 3
- key_weight: bfloat16 [512, 512], replicated, may hold values from -0.25 to 0.25
- value_weight: bfloat16 [512, 512], replicated, may hold values from -0.25 to 0.25
- value_bias: float32 [512], replicated, may hold values from -3 to 3
- projection_output_weight: bfloat16 [512, 512], replicated, may hold values from -1.5 to 1.5
- projection_output_bias: float32 [512], replicated, may hold values from -3 to 3
- cotangent: bfloat16 [64, 12, 12, 512], P('dp', 'row'), may hold values from -6 to 6
Outputs:
- decoded: bfloat16 [64, 12, 12, 512], P('dp', 'row')
- latent_grad: float32 [64, 12, 12, 256], P('dp', 'row')
- codebook_grad: float32 [16384, 256], P(('row', 'dp'))
- post_weight_grad: float32 [256, 256], P('dp')
- post_bias_grad: float32 [256], P('dp')
- entry_weight_grad: float32 [9, 256, 512], P(None, 'dp')
- entry_bias_grad: float32 [512], P('dp')
- first_gain_grad: float32 [512], P('dp')
- first_shift_grad: float32 [512], P('dp')
- first_weight_grad: float32 [9, 512, 512], P(None, 'dp')
- first_bias_grad: float32 [512], P('dp')
- second_gain_grad: float32 [512], P('dp')
- second_shift_grad: float32 [512], P('dp')
- second_weight_grad: float32 [9, 512, 512], P(None, 'dp')
- second_bias_grad: float32 [512], P('dp')
- mixer_gain_grad: float32 [512], P('dp')
- mixer_shift_grad: float32 [512], P('dp')
- query_weight_grad: float32 [512, 512], P('dp')
- query_bias_grad: float32 [512], P('dp')
- key_weight_grad: float32 [512, 512], P('dp')
- value_weight_grad: float32 [512, 512], P('dp')
- value_bias_grad: float32 [512], P('dp')
- output_weight_grad: float32 [512, 512], P('dp')
- output_bias_grad: float32 [512], P('dp')
The draws below stay inside these ranges and needn't reach their ends.
Inputs may be any that keep to these rules, and one draw needn't show every extreme that they name: `codes`: one code index for every latent position.
All inputs are finite; a program needn't handle non-finite values.
Results may differ from the reference program's by a relative error of at most 0.023.
Values may be sent and summed in bfloat16 or wider, within the bound.
No kernel may reach another device: no remote copies, remote signals or barrier semaphores. Data moves between devices by JAX's collectives and lax.ppermute only.
A program may use at most 128 MiB of HBM per device.

```python
import jax
import jax.numpy as jnp
from jax import lax

K = 16384
EMBED = 256
CH = 512
GROUPS = 32
LAT_H = 12
LAT_W = 12
BATCH = 64


def with_ends(values, key, smallest, largest):
    extent = values.shape
    spot = [jax.random.randint(jax.random.fold_in(key, axis), (), 0, extent[axis]) for axis in range(len(extent))]
    values = values.at[tuple(spot)].set(smallest)
    longest = extent.index(max(extent))
    spot[longest] = (spot[longest] + 1) % extent[longest]
    return values.at[tuple(spot)].set(largest)


def shard_levels(key, extent, cuts, smallest, high):
    loudness = 1.0
    for position, blocks in cuts:
        draws = jax.random.uniform(jax.random.fold_in(jax.random.fold_in(key, 6), position), (blocks,), jnp.float32, smallest / len(cuts), high / len(cuts))
        loudness = loudness * jnp.repeat(jnp.exp(draws), extent[position] // blocks).reshape((-1,) + (1,) * (len(extent) - 1 - position))
    return loudness


def gaussian(rng, shape, width, limit, split=(), kind=jnp.bfloat16):
    result = jax.random.normal(rng, shape, jnp.float32) * width
    if len(split) > 0:
        result = shard_levels(rng, shape, split, -0.22, 0.18) * result
    return jnp.clip(result, min=-limit, max=limit).astype(kind)


def setup_inputs(seed: int = 0) -> dict:
    key_of = jax.random.split(jax.random.key(seed), 26)
    latent = gaussian(key_of[0], (BATCH, LAT_H, LAT_W, EMBED), 1.0, 6.0, ((0, 8), (1, 4)))
    codes = with_ends(jax.random.randint(key_of[1], (BATCH, LAT_H, LAT_W), 0, K), jax.random.fold_in(key_of[1], 1), 0, K - 1).astype(jnp.int32)
    codebook = gaussian(key_of[2], (K, EMBED), 1.0, 6.0, ((0, 4),))
    post_weight = gaussian(key_of[3], (EMBED, EMBED), EMBED ** -0.5, 0.375)
    post_bias = gaussian(key_of[4], (EMBED,), 0.5, 3.0, (), jnp.float32)
    entry_weight = gaussian(key_of[5], (9, EMBED, CH), (9 * EMBED) ** -0.5, 0.125)
    entry_bias = gaussian(key_of[6], (CH,), 0.5, 3.0, (), jnp.float32)
    first_gain = jnp.clip(1.0 + 0.15 * jax.random.normal(key_of[7], (CH,), jnp.float32), 0.25, 1.75)
    first_shift = gaussian(key_of[8], (CH,), 0.5, 3.0, (), jnp.float32)
    first_weight = gaussian(key_of[9], (9, CH, CH), (9 * CH) ** -0.5, 0.09375)
    first_bias = gaussian(key_of[10], (CH,), 0.5, 3.0, (), jnp.float32)
    second_gain = jnp.clip(1.0 + 0.15 * jax.random.normal(key_of[11], (CH,), jnp.float32), 0.25, 1.75)
    second_shift = gaussian(key_of[12], (CH,), 0.5, 3.0, (), jnp.float32)
    second_weight = gaussian(key_of[13], (9, CH, CH), (9 * CH) ** -0.5, 0.09375)
    second_bias = gaussian(key_of[14], (CH,), 0.5, 3.0, (), jnp.float32)
    mixer_gain = jnp.clip(1.0 + 0.15 * jax.random.normal(key_of[15], (CH,), jnp.float32), 0.25, 1.75)
    mixer_shift = gaussian(key_of[16], (CH,), 0.5, 3.0, (), jnp.float32)
    query_weight = gaussian(key_of[17], (CH, CH), CH ** -0.5, 0.25)
    query_bias = gaussian(key_of[18], (CH,), 0.5, 3.0, (), jnp.float32)
    key_weight = gaussian(key_of[19], (CH, CH), CH ** -0.5, 0.25)
    value_weight = gaussian(key_of[20], (CH, CH), CH ** -0.5, 0.25)
    value_bias = gaussian(key_of[21], (CH,), 0.5, 3.0, (), jnp.float32)
    projection_output_weight = gaussian(key_of[22], (CH, CH), (CH // 32) ** -0.5, 1.5)
    projection_output_bias = gaussian(key_of[23], (CH,), 0.5, 3.0, (), jnp.float32)
    cotangent = gaussian(key_of[24], (BATCH, LAT_H, LAT_W, CH), 1.0, 6.0, ((0, 8), (1, 4)))
    return {"latent": latent, "codes": codes, "codebook": codebook, "post_weight": post_weight, "post_bias": post_bias, "entry_weight": entry_weight, "entry_bias": entry_bias, "first_gain": first_gain, "first_shift": first_shift, "first_weight": first_weight, "first_bias": first_bias, "second_gain": second_gain, "second_shift": second_shift, "second_weight": second_weight, "second_bias": second_bias, "mixer_gain": mixer_gain, "mixer_shift": mixer_shift, "query_weight": query_weight, "query_bias": query_bias, "key_weight": key_weight, "value_weight": value_weight, "value_bias": value_bias, "projection_output_weight": projection_output_weight, "projection_output_bias": projection_output_bias, "cotangent": cotangent}


@jax.custom_vjp
def reduced_precision(v):
    return lax.optimization_barrier(v.astype(jnp.bfloat16)).astype(jnp.float32)

@jax.custom_vjp
def reduced_backward(v):
    return v

def low_keep(v):
    return (reduced_precision(v), None)

def low_pass(kept, grad):
    return (grad,)

def back_keep(v):
    return (v, None)

def back_low(kept, grad):
    return (reduced_precision(grad),)
reduced_precision.defvjp(low_keep, low_pass)
reduced_backward.defvjp(back_keep, back_low)
EPSILON = 1e-06
BETA_COMMIT = 0.25
TOP_PRECISION = lax.Precision.HIGHEST

def group_norm(tensor, gain_vec, shift_vec):
    batch_size, rows_total, cols_total, channel_count = tensor.shape
    grouped = tensor.reshape(batch_size, rows_total * cols_total, GROUPS, channel_count // GROUPS)
    average = lax.optimization_barrier(jnp.mean(grouped, axis=(1, 3), keepdims=True))
    variance = lax.optimization_barrier(jnp.mean(jnp.square(grouped - average), axis=(1, 3), keepdims=True))
    normal = ((grouped - average) * lax.rsqrt(variance + EPSILON)).reshape(tensor.shape)
    return normal * gain_vec + shift_vec

def convolve(tensor, kernel):
    tap_count, chan_in, chan_out = kernel.shape
    return lax.conv_general_dilated(tensor, kernel.reshape(3, 3, chan_in, chan_out), (1, 1), 'SAME', dimension_numbers=('NHWC', 'HWIO', 'NHWC'), precision=TOP_PRECISION)

def decoder(quantized, params):
    post_weight, post_bias, entry_weight, entry_bias, first_gain, first_shift, first_weight, first_bias, second_gain, second_shift, second_weight, second_bias, mixer_gain, mixer_shift, query_weight, query_bias, key_weight, value_weight, value_bias, projection_output_weight, projection_output_bias = params
    batch_size, rows_total, cols_total, embed_dim = quantized.shape
    post = reduced_precision(reduced_backward(jnp.einsum('bhwe,ef->bhwf', quantized, post_weight, precision=TOP_PRECISION) + post_bias))
    stream = reduced_backward(convolve(post, entry_weight) + entry_bias)
    act_one = reduced_precision(jax.nn.silu(group_norm(stream, first_gain, first_shift)))
    middle = reduced_backward(convolve(act_one, first_weight) + first_bias)
    act_two = reduced_precision(jax.nn.silu(group_norm(middle, second_gain, second_shift)))
    branch = reduced_backward(convolve(act_two, second_weight) + second_bias)
    hidden = stream + branch
    normed = reduced_precision(reduced_backward(group_norm(hidden, mixer_gain, mixer_shift)))
    channel_count = normed.shape[3]
    tokens = normed.reshape(batch_size, rows_total * cols_total, channel_count)
    query_rows = reduced_precision(reduced_backward(jnp.einsum('bsc,cd->bsd', tokens, query_weight, precision=TOP_PRECISION) + query_bias))
    key_matrix_rows = reduced_precision(reduced_backward(jnp.einsum('bsc,cd->bsd', tokens, key_weight, precision=TOP_PRECISION)))
    value_matrix_rows = reduced_precision(reduced_backward(jnp.einsum('bsc,cd->bsd', tokens, value_weight, precision=TOP_PRECISION) + value_bias))
    attention_logits = reduced_backward(channel_count ** (-0.5) * jnp.einsum('nsw,nlw->nsl', query_rows, key_matrix_rows, precision=TOP_PRECISION))
    peak = lax.optimization_barrier(jnp.max(attention_logits, axis=2, keepdims=True))
    exponents = jnp.exp(attention_logits - peak)
    attention_probs = reduced_precision(exponents / lax.optimization_barrier(jnp.sum(exponents, axis=2, keepdims=True)))
    attention_output = reduced_precision(reduced_backward(jnp.einsum('lah,lhy->lay', attention_probs, value_matrix_rows, precision=TOP_PRECISION)))
    final_output = reduced_precision(reduced_backward(jnp.einsum('pzn,nt->pzt', attention_output, projection_output_weight, precision=TOP_PRECISION) + projection_output_bias))
    return hidden + final_output.reshape(hidden.shape)

def reference(latent, codes, codebook, post_weight, post_bias, entry_weight, entry_bias, first_gain, first_shift, first_weight, first_bias, second_gain, second_shift, second_weight, second_bias, mixer_gain, mixer_shift, query_weight, query_bias, key_weight, value_weight, value_bias, projection_output_weight, projection_output_bias, cotangent):
    params = tuple((tensor.astype(jnp.float32) for tensor in (post_weight, post_bias, entry_weight, entry_bias, first_gain, first_shift, first_weight, first_bias, second_gain, second_shift, second_weight, second_bias, mixer_gain, mixer_shift, query_weight, query_bias, key_weight, value_weight, value_bias, projection_output_weight, projection_output_bias)))
    book_float = codebook.astype(jnp.float32)
    latent_float = latent.astype(jnp.float32)
    code_list = codes.reshape(-1).astype(jnp.int32)
    quant_fixed = jnp.take(book_float, code_list, axis=0).reshape(latent.shape)

    def forward(quantized, book_rows, latent_vals, weight_set):
        looked = reduced_backward(jnp.take(book_rows, code_list, axis=0).reshape(latent.shape))
        loss = jnp.sum(jnp.square(looked - latent_float)) + BETA_COMMIT * jnp.sum(jnp.square(latent_vals - quant_fixed))
        return (decoder(quantized, weight_set), loss)
    (decoded, loss), pullback = jax.vjp(forward, quant_fixed, book_float, latent_float, params)
    grad_quant, grad_book, grad_latent, grad_params = pullback((cotangent.astype(jnp.float32), jnp.ones((), jnp.float32)))
    return (decoded.astype(jnp.bfloat16), grad_quant + grad_latent, grad_book, grad_params[0], grad_params[1], grad_params[2], grad_params[3], grad_params[4], grad_params[5], grad_params[6], grad_params[7], grad_params[8], grad_params[9], grad_params[10], grad_params[11], grad_params[12], grad_params[13], grad_params[14], grad_params[15], grad_params[16], grad_params[17], grad_params[18], grad_params[19], grad_params[20])
```

```python
import jax
import jax.numpy as jnp
from jax import lax
from jax.sharding import PartitionSpec as P

GROUPS = 32
EPSILON = 1e-06
BETA_COMMIT = 0.25
F32 = jnp.float32
BF16 = jnp.bfloat16


def bfloat(tensor):
    return tensor.astype(BF16)


def rounded(tensor):
    return lax.reduce_precision(tensor, 8, 7).astype(BF16)


def to_images(tensor):
    return lax.all_to_all(tensor, "row", split_axis=0, concat_axis=1, tiled=True)


def to_rows(tensor):
    return lax.all_to_all(tensor, "row", split_axis=1, concat_axis=0, tiled=True)


def gather_rows(tensor):
    count = lax.axis_size("row")
    copies = jnp.broadcast_to(tensor[None], (count,) + tensor.shape)
    got = lax.all_to_all(copies, "row", split_axis=0, concat_axis=0, tiled=True)
    got = jnp.moveaxis(got, 0, 1)
    return got.reshape((tensor.shape[0], count * tensor.shape[1]) + tensor.shape[2:])


def reduce_dp(blocks):
    count, rows, lanes = blocks.shape
    core = lax.rem(lax.axis_index("dp"), 2)
    pairs = bfloat(blocks).reshape(count // 2, 2, rows, lanes)
    mine = lax.dynamic_index_in_dim(pairs, core, 1, keepdims=False)
    other = lax.dynamic_index_in_dim(pairs, 1 - core, 1, keepdims=False)
    got = lax.ppermute(other, "dp", [(i, i ^ 1) for i in range(count)])
    both = bfloat(mine.astype(F32) + got.astype(F32))
    groups = [[2 * i + c for i in range(count // 2)] for c in range(2)]
    parts = lax.all_to_all(both, "dp", 0, 0, axis_index_groups=groups, tiled=True)
    return jnp.sum(parts.astype(F32), axis=0)


def reduce_row(part):
    count = lax.axis_size("row")
    me = lax.axis_index("row")
    half = count // 2
    for k in range(half - 1):
        got = lax.ppermute(rounded(part), "row", [(k, k + 1), (count - 1 - k, count - 2 - k)])
        part = part + got.astype(F32)
    low = rounded(part)
    got = lax.ppermute(low, "row", [(half - 1, half), (half, half - 1)])
    total = rounded(low.astype(F32) + got.astype(F32))
    for k in range(half - 1, 0, -1):
        got = lax.ppermute(total, "row", [(k, k - 1), (count - 1 - k, count - k)])
        total = jnp.where((me == k - 1) | (me == count - k), got, total)
    return total.astype(F32)


def patches(tensor, reverse):
    height, width = tensor.shape[1], tensor.shape[2]
    padded = jnp.pad(tensor, ((0, 0), (1, 1), (1, 1), (0, 0)))
    tap_list = []
    for row_tap in range(3):
        for col_tap in range(3):
            y = 2 - row_tap if reverse else row_tap
            x = 2 - col_tap if reverse else col_tap
            tap_list.append(padded[:, y : y + height, x : x + width, :])
    return jnp.stack(tap_list, axis=3)


def conv_apply(columns, kernel):
    return jnp.einsum("bhwtc,tcf->bhwf", columns, kernel, preferred_element_type=F32)


def conv_back(columns, kernel):
    return jnp.einsum("bhwtf,tcf->bhwc", columns, kernel, preferred_element_type=F32)


def kernel_grad(columns, gradient):
    return jnp.einsum("bhwtc,bhwf->tcf", columns, gradient, preferred_element_type=F32)


def group_view(tensor):
    batch_size, height, width, channel_count = tensor.shape
    return tensor.reshape(batch_size, height * width, GROUPS, channel_count // GROUPS)


def group_stats(tensor):
    grouped = group_view(tensor)
    average = jnp.mean(grouped, axis=(1, 3))
    variance = jnp.mean(jnp.square(grouped - average[:, None, :, None]), axis=(1, 3))
    return (average, lax.rsqrt(variance + EPSILON))


def normalize(tensor, average, inverse):
    grouped = group_view(tensor)
    scaled = (grouped - average[:, None, :, None]) * inverse[:, None, :, None]
    return scaled.reshape(tensor.shape)


def norm_back(gradient, standard, inverse, gain_vec):
    gain_grad = jnp.sum(gradient * standard, axis=(0, 1, 2))
    shift_grad = jnp.sum(gradient, axis=(0, 1, 2))
    scaled = group_view(gradient * gain_vec)
    normal = group_view(standard)
    first = jnp.mean(scaled, axis=(1, 3))
    second = jnp.mean(scaled * normal, axis=(1, 3))
    out = (scaled - first[:, None, :, None] - normal * second[:, None, :, None]) * inverse[
        :, None, :, None
    ]
    return (out.reshape(gradient.shape), gain_grad, shift_grad)


def silu_slope(pre_act):
    logistic = jax.nn.sigmoid(pre_act)
    return logistic * (1.0 + pre_act * (1.0 - logistic))


def mm(pattern, a, b):
    return jnp.einsum(pattern, a, b, preferred_element_type=F32)


def on_device(
    latent,
    codes,
    codebook,
    post_weight,
    post_bias,
    entry_weight,
    entry_bias,
    first_gain,
    first_shift,
    first_weight,
    first_bias,
    second_gain,
    second_shift,
    second_weight,
    second_bias,
    mixer_gain,
    mixer_shift,
    query_weight,
    query_bias,
    key_weight,
    value_weight,
    value_bias,
    projection_output_weight,
    projection_output_bias,
    cotangent,
):
    batch, rows_local, width, embed = latent.shape
    channels = entry_weight.shape[2]
    row_count = lax.axis_size("row")
    dp_count = lax.axis_size("dp")
    owned = codebook.shape[0]
    height = rows_local * row_count
    crops = batch // row_count
    sequence = height * width
    tokens_all = batch * sequence
    me = lax.axis_index("row")

    all_codes = lax.all_gather(codes, "row", axis=1, tiled=True).reshape(tokens_all)
    one_hot = (
        all_codes[:, None] - me * owned == lax.broadcasted_iota(jnp.int32, (tokens_all, owned), 1)
    ).astype(BF16)
    found = bfloat(jnp.dot(one_hot, codebook, preferred_element_type=F32))
    pieces = lax.all_to_all(
        found.reshape(row_count, crops * sequence, embed), "row", 0, 0, tiled=True
    )
    quant = bfloat(jnp.sum(pieces.astype(F32), axis=0))
    cot = to_images(cotangent)
    latent_all = gather_rows(latent).reshape(tokens_all, embed)
    difference = bfloat(2.0 * (found.astype(F32) - latent_all.astype(F32)))
    grad_book = jnp.einsum("pk,pe->ke", one_hot, difference, preferred_element_type=F32)
    codebook_grad = lax.psum_scatter(bfloat(grad_book), "dp", scatter_dimension=0, tiled=True).astype(F32)
    latent_mine = lax.dynamic_slice_in_dim(latent_all, me * crops * sequence, crops * sequence, 0)

    post = bfloat(jnp.dot(quant, post_weight, preferred_element_type=F32) + post_bias).reshape(
        crops, height, width, embed
    )
    post_cols = patches(post, False)
    stream = conv_apply(post_cols, entry_weight) + entry_bias
    average_one, inverse_one = group_stats(stream)
    standard_one = normalize(stream, average_one, inverse_one)
    pre_one = standard_one * first_gain + first_shift
    cols_one = patches(bfloat(jax.nn.silu(pre_one)), False)
    middle = conv_apply(cols_one, first_weight) + first_bias
    average_two, inverse_two = group_stats(middle)
    standard_two = normalize(middle, average_two, inverse_two)
    pre_two = standard_two * second_gain + second_shift
    cols_two = patches(bfloat(jax.nn.silu(pre_two)), False)
    hidden = stream + (conv_apply(cols_two, second_weight) + second_bias)
    average_mix, inverse_mix = group_stats(hidden)
    standard_mix = normalize(hidden, average_mix, inverse_mix)
    tokens = bfloat(standard_mix * mixer_gain + mixer_shift).reshape(crops, sequence, channels)
    cot_seq = cot.reshape(crops, sequence, channels)
    query = bfloat(mm("bsc,cd->bsd", tokens, query_weight) + query_bias)
    key = bfloat(mm("bsc,cd->bsd", tokens, key_weight))
    value = bfloat(mm("bsc,cd->bsd", tokens, value_weight) + value_bias)
    scale = channels ** (-0.5)
    logits = mm("nsw,nlw->nsl", query, key) * scale
    peak = jnp.max(logits, axis=2, keepdims=True)
    exponents = jnp.exp(logits - peak)
    probs = exponents / jnp.sum(exponents, axis=2, keepdims=True)
    weights = bfloat(probs)
    attended = bfloat(mm("nsl,nlw->nsw", weights, value))
    result = bfloat(mm("nsw,wt->nst", attended, projection_output_weight) + projection_output_bias)
    decoded = to_rows(bfloat(hidden + result.astype(F32).reshape(hidden.shape)))

    grad_output_weight = mm("nst,nsx->tx", attended, cot_seq)
    grad_output_bias = jnp.sum(cot_seq.astype(F32), axis=(0, 1))
    grad_attended = bfloat(mm("nsu,iu->nsi", cot_seq, projection_output_weight))
    grad_weights = mm("nsw,nlw->nsl", grad_attended, value)
    grad_value = bfloat(mm("nsl,nsw->nlw", weights, grad_attended))
    grad_scores = bfloat(
        probs * (grad_weights - jnp.sum(grad_weights * probs, axis=2, keepdims=True))
    )
    grad_query = bfloat(mm("nsl,nlw->nsw", grad_scores, key) * scale)
    grad_key = bfloat(mm("nsl,nsw->nlw", grad_scores, query) * scale)
    grad_query_weight = mm("bsc,bsd->cd", tokens, grad_query)
    grad_query_bias = jnp.sum(grad_query.astype(F32), axis=(0, 1))
    grad_key_weight = mm("bsc,bsd->cd", tokens, grad_key)
    grad_value_weight = mm("bsc,bsd->cd", tokens, grad_value)
    grad_value_bias = jnp.sum(grad_value.astype(F32), axis=(0, 1))
    grad_tokens = (
        mm("bsd,cd->bsc", grad_query, query_weight)
        + mm("bsd,cd->bsc", grad_key, key_weight)
        + mm("bsd,cd->bsc", grad_value, value_weight)
    )
    grad_normed = bfloat(grad_tokens).reshape(hidden.shape).astype(F32)
    grad_mix, grad_mixer_gain, grad_mixer_shift = norm_back(
        grad_normed, standard_mix, inverse_mix, mixer_gain
    )
    grad_hidden = cot.astype(F32) + grad_mix
    grad_branch = bfloat(grad_hidden)
    grad_second_weight = kernel_grad(cols_two, grad_branch)
    grad_second_bias = jnp.sum(grad_branch.astype(F32), axis=(0, 1, 2))
    grad_act_two = conv_back(patches(grad_branch, True), second_weight)
    grad_middle_full, grad_second_gain, grad_second_shift = norm_back(
        grad_act_two * silu_slope(pre_two), standard_two, inverse_two, second_gain
    )
    grad_middle = bfloat(grad_middle_full)
    grad_first_weight = kernel_grad(cols_one, grad_middle)
    grad_first_bias = jnp.sum(grad_middle.astype(F32), axis=(0, 1, 2))
    grad_act_one = conv_back(patches(grad_middle, True), first_weight)
    grad_stream_norm, grad_first_gain, grad_first_shift = norm_back(
        grad_act_one * silu_slope(pre_one), standard_one, inverse_one, first_gain
    )
    grad_stream = bfloat(grad_hidden + grad_stream_norm)
    grad_entry_weight = kernel_grad(post_cols, grad_stream)
    grad_entry_bias = jnp.sum(grad_stream.astype(F32), axis=(0, 1, 2))
    grad_post = bfloat(conv_back(patches(grad_stream, True), entry_weight)).reshape(
        crops * sequence, embed
    )
    grad_post_weight = mm("pe,pf->ef", quant, grad_post)
    grad_post_bias = jnp.sum(grad_post.astype(F32), axis=0)
    grad_latent = mm("pf,ef->pe", grad_post, post_weight) + 2.0 * BETA_COMMIT * (
        latent_mine.astype(F32) - quant.astype(F32)
    )
    latent_grad = to_rows(bfloat(grad_latent).reshape(crops, height, width, embed)).astype(F32)

    def taps(grad):
        count, inner, outer = grad.shape
        return (
            grad.reshape(count, dp_count, inner // dp_count, outer)
            .transpose(1, 0, 2, 3)
            .reshape(dp_count, count * inner // dp_count, outer)
        )

    def whole(grad):
        return grad.reshape(dp_count, -1, channels)

    vectors = jnp.concatenate(
        [
            v.reshape(dp_count, -1)
            for v in (
                grad_entry_bias,
                grad_first_gain,
                grad_first_shift,
                grad_first_bias,
                grad_second_gain,
                grad_second_shift,
                grad_second_bias,
                grad_mixer_gain,
                grad_mixer_shift,
                grad_query_bias,
                grad_value_bias,
                grad_output_bias,
                grad_post_bias,
            )
        ],
        axis=1,
    )
    size = vectors.shape[1]
    lines = -(-size // channels)
    vectors = jnp.pad(vectors, ((0, 0), (0, lines * channels - size))).reshape(
        dp_count, lines, channels
    )

    parts_a = [whole(g) for g in (grad_output_weight, grad_query_weight, grad_key_weight, grad_value_weight)]
    parts_a.append(taps(grad_second_weight))
    sum_a = reduce_row(reduce_dp(jnp.concatenate(parts_a, axis=1)))
    sum_b = reduce_row(reduce_dp(taps(grad_first_weight)))
    parts_c = [taps(grad_entry_weight), whole(grad_post_weight), vectors]
    sum_c = reduce_row(reduce_dp(jnp.concatenate(parts_c, axis=1)))

    share = channels // dp_count
    o_w, q_w, k_w, v_w = (sum_a[i * share : (i + 1) * share] for i in range(4))
    second_w = sum_a[4 * share :].reshape(9, share, channels)
    first_w = sum_b.reshape(9, share, channels)
    e_share = embed // dp_count
    entry_w = sum_c[: 9 * e_share].reshape(9, e_share, channels)
    post_rows = e_share * embed // channels
    post_w = sum_c[9 * e_share : 9 * e_share + post_rows].reshape(e_share, embed)
    flat = sum_c[9 * e_share + post_rows :].reshape(-1)
    vec = [flat[i * share : (i + 1) * share] for i in range(12)]
    post_b = flat[12 * share : 12 * share + e_share]
    return (
        decoded,
        latent_grad,
        codebook_grad,
        post_w,
        post_b,
        entry_w,
        vec[0],
        vec[1],
        vec[2],
        first_w,
        vec[3],
        vec[4],
        vec[5],
        second_w,
        vec[6],
        vec[7],
        vec[8],
        q_w,
        vec[9],
        k_w,
        v_w,
        vec[10],
        o_w,
        vec[11],
    )


def solution(mesh):
    def cells(depth):
        return P("dp", "row", *([None] * depth))

    return jax.shard_map(
        on_device,
        mesh=mesh,
        in_specs=(cells(2), cells(1), P("row", None)) + (P(),) * 21 + (cells(2),),
        out_specs=(
            cells(2),
            cells(2),
            P(("row", "dp"), None),
            P("dp", None),
            P("dp"),
            P(None, "dp", None),
            P("dp"),
            P("dp"),
            P("dp"),
            P(None, "dp", None),
            P("dp"),
            P("dp"),
            P("dp"),
            P(None, "dp", None),
            P("dp"),
            P("dp"),
            P("dp"),
            P("dp", None),
            P("dp"),
            P("dp", None),
            P("dp", None),
            P("dp"),
            P("dp", None),
            P("dp"),
        ),
        check_vma=False,
    )
```

```python
import functools

import jax
import jax.numpy as jnp
from jax import lax
from jax.experimental import pallas as pl
from jax.experimental.pallas import tpu as pltpu
from jax.sharding import PartitionSpec as P

GROUPS = 32
EPSILON = 1e-06
BETA_COMMIT = 0.25
F32 = jnp.float32
BF16 = jnp.bfloat16
VMEM_BYTES = 56 * 1024 * 1024
PACE = 1.15
SMALL = 12 * 1024 * 1024
VMEM = pl.BlockSpec(memory_space=pltpu.VMEM)
ANY = pl.BlockSpec(memory_space=pl.ANY)
SMEM = pl.BlockSpec(memory_space=pltpu.SMEM)


def bfloat(tensor):
    return tensor.astype(BF16)


def rounded(tensor):
    return lax.reduce_precision(tensor, 8, 7).astype(BF16)


def dot(a, b):
    return lax.dot_general(a, b, (((1,), (0,)), ((), ())), preferred_element_type=F32)


def dot_nt(a, b):
    return lax.dot_general(a, b, (((1,), (1,)), ((), ())), preferred_element_type=F32)


def dot_tn(a, b):
    return lax.dot_general(a, b, (((0,), (0,)), ((), ())), preferred_element_type=F32)


def same_group(channels):
    width = channels // GROUPS
    row = lax.broadcasted_iota(jnp.int32, (channels, channels), 0) // width
    col = lax.broadcasted_iota(jnp.int32, (channels, channels), 1) // width
    return (row == col).astype(F32).astype(BF16)


def stacked(rows):
    place = lax.broadcasted_iota(jnp.int32, (8, rows[0].shape[1]), 0)
    out = jnp.zeros((8, rows[0].shape[1]), F32)
    for i, row in enumerate(rows):
        out = jnp.where(place == i, row, out)
    return out


def group_sums(rows, group):
    high = bfloat(rows).astype(F32)
    rest = rows - high
    mid = bfloat(rest).astype(F32)
    parts = bfloat(jnp.concatenate([high, mid, rest - mid], axis=0))
    sums = dot(parts, group)
    return sums[0:8] + sums[8:16] + sums[16:24]


def by_crop(tensor, crops):
    size = tensor.shape[0] // crops
    return [tensor[i * size : (i + 1) * size] for i in range(crops)]


def total(tensor):
    return jnp.sum(tensor, axis=0, keepdims=True)


def norm(tensor, group, crops):
    parts = by_crop(tensor, crops)
    members = parts[0].shape[0] * (tensor.shape[1] // GROUPS)
    means = group_sums(stacked([total(p) for p in parts]), group) * (1.0 / members)
    parts = [p - means[i : i + 1] for i, p in enumerate(parts)]
    spread = group_sums(stacked([total(p * p) for p in parts]), group) * (1.0 / members)
    inverse = lax.rsqrt(spread + EPSILON)
    standard = jnp.concatenate([p * inverse[i : i + 1] for i, p in enumerate(parts)], axis=0)
    return standard, inverse


def norm_back(grad, standard, inverse, gain, group, crops):
    grads, normals = by_crop(grad, crops), by_crop(standard, crops)
    members = grads[0].shape[0] * (grad.shape[1] // GROUPS)
    firsts = [total(g) for g in grads]
    seconds = [total(g * n) for g, n in zip(grads, normals)]
    means = group_sums(stacked([v * gain for v in firsts + seconds]), group) * (1.0 / members)
    outs = [
        (g * gain - means[i : i + 1] - n * means[crops + i : crops + i + 1]) * inverse[i : i + 1]
        for i, (g, n) in enumerate(zip(grads, normals))
    ]
    return jnp.concatenate(outs, axis=0), sum(seconds[1:], seconds[0]), sum(firsts[1:], firsts[0])


def spread_taps(out_ref, tensor, mask_ref, width, sign):
    rows, lanes = tensor.shape
    for tap in range(9):
        step = sign * ((tap // 3 - 1) * width + tap % 3 - 1)
        moved = tensor
        if step:
            seen = tap if sign > 0 else 8 - tap
            moved = pltpu.roll(tensor, (-step) % rows, 0) * mask_ref[:, seen : seen + 1]
        out_ref[:, tap * lanes : (tap + 1) * lanes] = bfloat(moved)


def tap_masks(crops, height, width):
    y = jnp.arange(height).reshape(1, height, 1, 1)
    x = jnp.arange(width).reshape(1, 1, width, 1)
    tap = jnp.arange(16).reshape(1, 1, 1, 16)
    dy, dx = tap // 3 - 1, tap % 3 - 1
    fits = (y + dy >= 0) & (y + dy < height) & (x + dx >= 0) & (x + dx < width)
    return jnp.broadcast_to(fits, (crops, height, width, 16)).reshape(-1, 16).astype(F32)


def silu_slope(pre_act):
    logistic = jax.nn.sigmoid(pre_act)
    return logistic * (1.0 + pre_act * (1.0 - logistic))


def fetch(sources, buffers, sems):
    copies = [
        pltpu.make_async_copy(s, b, sems.at[i]) for i, (s, b) in enumerate(zip(sources, buffers))
    ]
    for copy in copies:
        copy.start()
    return copies


def cost(micros):
    return pl.CostEstimate(flops=int(micros * PACE * 1e9), bytes_accessed=0, transcendentals=0)


def call(kernel, inputs, outputs, scratch, micros, limit=VMEM_BYTES):
    return pl.pallas_call(
        kernel,
        out_shape=[jax.ShapeDtypeStruct(s, d) for s, d in outputs],
        in_specs=[s for _, s in inputs],
        out_specs=[VMEM] * len(outputs),
        scratch_shapes=scratch,
        cost_estimate=cost(micros),
        compiler_params=pltpu.CompilerParams(vmem_limit_bytes=limit),
    )(*[a for a, _ in inputs])


def to_crops(tensor, crops, count):
    part = tensor.shape[0] // (crops * count)
    return jnp.concatenate(
        [tensor[(s * crops + c) * part : (s * crops + c + 1) * part] for c in range(crops) for s in range(count)], axis=0
    )


def to_slabs(tensor, crops, count):
    part = tensor.shape[0] // (crops * count)
    return jnp.concatenate(
        [tensor[(c * count + s) * part : (c * count + s + 1) * part] for s in range(count) for c in range(crops)], axis=0
    )


def put_blocks(out, place, tensor):
    chips, _, lanes = out.shape
    lanes //= 3
    share = tensor.shape[1] // chips
    for i in range(chips):
        block = tensor[:, i * share : (i + 1) * share]
        if share < lanes:
            block = jnp.concatenate([block, jnp.zeros((tensor.shape[0], lanes - share), block.dtype)], axis=1)
        out[i, :, place * lanes : (place + 1) * lanes] = block


def late_kernel(array, after, out):
    out[...] = array[...]


def late(array, after):
    return call(late_kernel, [(array, VMEM), (after, ANY)], [(array.shape, array.dtype)], [], 0.1, SMALL)[0]


def lookup_kernel(count, me_i, *refs):
    codes, book, found_o, refs = refs[:count], refs[count], refs[count + 1], refs[count + 2 :]
    outs, (one_hot, held) = refs[:count], refs[count:]
    owned = book.shape[0]
    size = codes[0].shape[1]
    me = me_i[0, 0]
    lane = lax.broadcasted_iota(jnp.int32, (size, 128), 1)
    for k in range(count):
        wanted = codes[k][...] - me * owned
        wanted = jnp.transpose(jnp.broadcast_to(wanted, (128, size)), (1, 0)) - lane
        for start in range(0, owned, 128):
            one_hot[k * size : (k + 1) * size, start : start + 128] = bfloat((wanted == start).astype(F32))
    found = dot(one_hot[...], book[...])
    held[...] = found
    found_o[...] = bfloat(found)
    part = size // count
    for k in range(count):
        rows = [
            held[pl.ds(pl.multiple_of((s ^ me) * size + (me ^ k) * part, 8), part), :] for s in range(count)
        ]
        outs[k][...] = bfloat(jnp.concatenate(rows, axis=0))


def lookup(me, codes, book):
    count, size, embed = len(codes), codes[0].shape[1], book.shape[1]
    return call(
        functools.partial(lookup_kernel, count),
        [(me, SMEM)] + [(c, VMEM) for c in codes] + [(book, VMEM)],
        [((count * size, embed), BF16)] + [((size, embed), BF16)] * count,
        [pltpu.VMEM((count * size, book.shape[0]), BF16), pltpu.VMEM((count * size, embed), F32)],
        5.4,
    )


def scatter_kernel(count, me_i, *refs):
    codes, latents, found, core_i = refs[:count], refs[count : 2 * count], refs[2 * count], refs[2 * count + 1]
    mine, other, gaps, sums_s = refs[-4:]
    chips, rows, _ = mine.shape
    owned = 2 * chips * rows
    core = core_i[0, 0]
    size = codes[0].shape[1]
    me = me_i[0, 0]
    for k in range(count):
        latent = latents[k][...].astype(F32)
        here = slice(k * size, (k + 1) * size)
        gaps[here, :] = bfloat(2.0 * (found[here, :].astype(F32) - latent))
    block = max(2 * rows, 1024)
    row = lax.broadcasted_iota(jnp.int32, (block, size), 0)
    for start in range(0, owned, block):
        one_hot = [bfloat((row == codes[k][...] - (me * owned + start)).astype(F32)) for k in range(count)]
        sums = dot(one_hot[0], gaps[:size, :])
        for k in range(1, count):
            sums = sums + dot(one_hot[k], gaps[k * size : (k + 1) * size, :])
        sums_s[...] = sums
        for d in range(block // (2 * rows)):
            for out, half in ((mine, core), (other, 1 - core)):
                here = pl.ds(pl.multiple_of((2 * d + half) * rows, 8), rows)
                out[start // (2 * rows) + d] = bfloat(sums_s[here, :])


def scatter(me, core, codes, latents, found, owned, chips, afters):
    count, size, embed = len(codes), codes[0].shape[1], found.shape[1]
    return call(
        functools.partial(scatter_kernel, count),
        [(me, SMEM)]
        + [(a, VMEM) for a in (*codes, *latents, found)]
        + [(core, SMEM)]
        + [(a, ANY) for a in afters],
        [((chips, owned // (2 * chips), embed), BF16)] * 2,
        [
            pltpu.VMEM((count * size, embed), BF16),
            pltpu.VMEM((max(owned // chips, 1024), embed), F32),
        ],
        5.0,
    )


def forward_kernel(crops, width, count, *refs):
    pieces, refs = refs[:count], refs[count:]
    (
        masks, post_w, post_b, entry_b, gain_1, shift_1, bias_1, gain_2, shift_2, bias_2, gain_m, shift_m, q_b, v_b, o_b,
        *refs,
    ) = refs
    sources, refs = refs[:7], refs[7:]
    (
        quant_o, acts_o, normed_o, attended_o, decoded_o, standard_1, standard_2, standard_m, inverses,
        query_o, key_o, value_o, probs_o, *refs,
    ) = refs
    entry_w, first_w, second_w, q_w, k_w, v_w, o_w, columns, hidden_s, sems = refs
    copies = fetch(sources, refs[:7], sems)
    channels = entry_w.shape[1]
    rows = quant_o.shape[0]
    size = rows // crops
    scale = channels ** (-0.5)
    found = pieces[0][...].astype(F32)
    for piece in pieces[1:]:
        found = found + piece[...].astype(F32)
    quant = bfloat(to_crops(found, crops, count))
    quant_o[...] = quant
    post = bfloat(dot(quant, post_w[...]) + post_b[...])
    put_blocks(acts_o, 2, post)
    embed = post.shape[1]
    spread_taps(columns.at[:, : 9 * embed], post.astype(F32), masks, width, 1)
    group = same_group(channels)
    copies[0].wait()
    stream = dot(columns[:, : 9 * embed], entry_w[...]) + entry_b[...]
    hidden_s[...] = stream
    standard, inverse = norm(stream, group, crops)
    standard_1[...] = standard
    inverses[0] = inverse
    act = bfloat(jax.nn.silu(standard * gain_1[...] + shift_1[...]))
    put_blocks(acts_o, 1, act)
    spread_taps(columns, act.astype(F32), masks, width, 1)
    copies[1].wait()
    middle = dot(columns[...], first_w[...].reshape(9 * channels, channels)) + bias_1[...]
    standard, inverse = norm(middle, group, crops)
    standard_2[...] = standard
    inverses[1] = inverse
    act = bfloat(jax.nn.silu(standard * gain_2[...] + shift_2[...]))
    put_blocks(acts_o, 0, act)
    spread_taps(columns, act.astype(F32), masks, width, 1)
    copies[2].wait()
    hidden = hidden_s[...] + (dot(columns[...], second_w[...].reshape(9 * channels, channels)) + bias_2[...])
    hidden_s[...] = hidden
    standard, inverse = norm(hidden, group, crops)
    standard_m[...] = standard
    inverses[2] = inverse
    normed = bfloat(standard * gain_m[...] + shift_m[...])
    normed_o[...] = normed
    for copy in copies[3:]:
        copy.wait()
    query_o[...] = bfloat(dot(normed, q_w[...]) + q_b[...])
    key_o[...] = bfloat(dot(normed, k_w[...]))
    value_o[...] = bfloat(dot(normed, v_w[...]) + v_b[...])
    for i in range(crops):
        here = slice(i * size, (i + 1) * size)
        logits = dot_nt(query_o[here, :], key_o[here, :]) * scale
        exponents = jnp.exp(logits - jnp.max(logits, axis=1, keepdims=True))
        probs = exponents / jnp.sum(exponents, axis=1, keepdims=True)
        probs_o[i] = probs
        attended_o[here, :] = bfloat(dot(bfloat(probs), value_o[here, :]))
    result = bfloat(dot(attended_o[...], o_w[...]) + o_b[...])
    decoded_o[...] = bfloat(to_slabs(hidden_s[...] + result.astype(F32), crops, count))


def forward(crops, width, pieces, masks, post_w, vectors, weights, chips):
    rows, embed = pieces[0].shape
    channels = weights[0].shape[2]
    wide = (rows, channels)
    lanes = 3 * (-(-channels // chips // 128) * 128)
    buffers = [w.reshape(-1, channels) if w.shape[1] == embed else w for w in weights]
    return call(
        functools.partial(forward_kernel, crops, width, len(pieces)),
        [(a, VMEM) for a in (*pieces, masks, post_w)]
        + [(v.reshape(1, -1), VMEM) for v in vectors]
        + [(w, ANY) for w in buffers],
        [((rows, embed), BF16), ((chips, rows, lanes), BF16)]
        + [(wide, BF16)] * 3
        + [(wide, F32)] * 3
        + [((3, 8, channels), F32)]
        + [(wide, BF16)] * 3
        + [((crops, rows // crops, rows // crops), F32)],
        [pltpu.VMEM(w.shape, BF16) for w in buffers]
        + [
            pltpu.VMEM((rows, 9 * channels), BF16),
            pltpu.VMEM(wide, F32),
            pltpu.SemaphoreType.DMA((len(buffers),)),
        ],
        12.5,
    )


def backward_kernel(crops, width, count, *refs):
    (
        cot_i, masks, standard_1, standard_2, standard_m, inverses, query, key, value, probs_i,
        gain_1, shift_1, gain_2, shift_2, gain_m, after, *refs,
    ) = refs
    sources, refs = refs[:6], refs[6:]
    cot_o, grad_q_o, grad_k_o, grad_v_o, all_o, stream_o, vectors_o, *refs = refs
    o_w, q_w, k_w, v_w, second_w, first_w, columns, hidden_s, sems = refs
    copies = fetch(sources, refs[:6], sems)
    rows, channels = query.shape
    size = rows // crops
    scale = channels ** (-0.5)
    group = same_group(channels)
    cot = bfloat(to_crops(cot_i[...].astype(F32), crops, count))
    cot_o[...] = cot
    copies[0].wait()
    grads_att = by_crop(bfloat(dot_nt(cot, o_w[...])), crops)
    for i in range(crops):
        here = slice(i * size, (i + 1) * size)
        grad_att, probs = grads_att[i], probs_i[i]
        grad_w = dot_nt(grad_att, value[here, :])
        grad_v_o[here, :] = bfloat(dot_tn(bfloat(probs), grad_att))
        grad_s = bfloat(probs * (grad_w - jnp.sum(grad_w * probs, axis=1, keepdims=True)))
        grad_q_o[here, :] = bfloat(dot(grad_s, key[here, :]) * scale)
        grad_k_o[here, :] = bfloat(dot_tn(grad_s, query[here, :]) * scale)
    grad_q, grad_k, grad_v = grad_q_o[...], grad_k_o[...], grad_v_o[...]
    for copy in copies[1:4]:
        copy.wait()
    grad_normed = bfloat(dot_nt(grad_q, q_w[...]) + dot_nt(grad_k, k_w[...]) + dot_nt(grad_v, v_w[...]))
    grad, gain_grad_m, shift_grad_m = norm_back(
        grad_normed.astype(F32), standard_m[...], inverses[2], gain_m[...], group, crops
    )
    grad = cot.astype(F32) + grad
    hidden_s[...] = grad
    branch = bfloat(grad)

    def through(grad, weight, standard_ref, inverse, gain_ref, shift_ref):
        grad = conv_back(grad, masks, width, weight, columns)
        standard, gain = standard_ref[...], gain_ref[...]
        grad = grad * silu_slope(standard * gain + shift_ref[...])
        return norm_back(grad, standard, inverse, gain, group, crops)

    copies[4].wait()
    grad, gain_grad_2, shift_grad_2 = through(branch, second_w, standard_2, inverses[1], gain_2, shift_2)
    middle = bfloat(grad)
    copies[5].wait()
    grad, gain_grad_1, shift_grad_1 = through(middle, first_w, standard_1, inverses[0], gain_1, shift_1)
    stream = bfloat(hidden_s[...] + grad)
    stream_o[...] = stream
    for i in range(all_o.shape[0]):
        all_o[i, :rows] = branch
        all_o[i, rows : 2 * rows] = middle
        all_o[i, 2 * rows :] = stream
    sums = [total(v.astype(F32)) for v in (stream, middle, grad_q, grad_v, cot, branch)]
    vectors_o[0:8] = stacked([gain_grad_1, shift_grad_1, sums[0], gain_grad_2, shift_grad_2, sums[1]])
    vectors_o[8:16] = stacked([gain_grad_m, shift_grad_m, *sums[2:]])


def backward(crops, width, count, chips, arrays, vectors, after, weights):
    rows, channels = arrays[0].shape
    wide = (rows, channels)
    return call(
        functools.partial(backward_kernel, crops, width, count),
        [(a, VMEM) for a in arrays]
        + [(v.reshape(1, -1), VMEM) for v in vectors]
        + [(after, ANY)]
        + [(w, ANY) for w in weights],
        [(wide, BF16)] * 4
        + [((chips, 3 * rows, channels), BF16), (wide, BF16), ((16, channels), F32)],
        [pltpu.VMEM(w.shape, BF16) for w in weights]
        + [
            pltpu.VMEM((rows, 9 * channels), BF16),
            pltpu.VMEM(wide, F32),
            pltpu.SemaphoreType.DMA((len(weights),)),
        ],
        11.0,
    )


def attention_grads_kernel(core_i, normed, attended, cot, grad_q, grad_k, grad_v, small_mine, small_other, *refs):
    mine, other, wide = refs[-3:]
    core = core_i[0, 0]
    channels = normed.shape[1]
    pairs = ((attended, cot), (normed, grad_q), (normed, grad_k), (normed, grad_v))
    share = (mine.shape[1] - small_mine.shape[1]) // len(pairs)
    mine[:, len(pairs) * share :] = small_mine[...]
    other[:, len(pairs) * share :] = small_other[...]
    for i, (a, b) in enumerate(pairs):
        wide[...] = dot_tn(a[...], b[...])
        for d in range(channels // (2 * share)):
            for out, half in ((mine, core), (other, 1 - core)):
                start = pl.multiple_of((2 * d + half) * share, 8)
                out[d, i * share : (i + 1) * share, :] = bfloat(wide[pl.ds(start, share), :])


def attention_grads(dp_count, core, arrays, afters):
    rows, channels = arrays[0].shape
    share = channels // dp_count
    out = ((dp_count // 2, 4 * share + arrays[-1].shape[1], channels), BF16)
    return call(
        attention_grads_kernel,
        [(core, SMEM)] + [(a, VMEM) for a in arrays] + [(a, ANY) for a in afters],
        [out, out],
        [pltpu.VMEM((channels, channels), F32)],
        4.0,
    )


def conv_back(grad, masks, width, weight, columns):
    lanes = grad.shape[1]
    spread_taps(columns, grad.astype(F32), masks, width, -1)
    out = dot_nt(columns[:, :lanes], weight[0])
    for tap in range(1, 9):
        out = out + dot_nt(columns[:, tap * lanes : (tap + 1) * lanes], weight[tap])
    return out


def post_kernel(
    crops, count, width, me_i, core_i, grad_i, masks, quant_i, post_w, vectors_i, decoded_i, *refs,
):
    weight_hbm, *refs = refs[-count - 8 :]
    backs, (mine, other, weight, columns, held, vectors, sems) = refs[:count], refs[count:]
    copies = fetch((weight_hbm,), (weight,), sems)
    copies[0].wait()
    grad_post = bfloat(conv_back(grad_i[...], masks, width, weight, columns))
    quant = quant_i[...]
    embed = quant.shape[1]
    grad_latent = dot_nt(grad_post, post_w[...]) - 2.0 * BETA_COMMIT * quant.astype(F32)
    channels = decoded_i.shape[1]
    held[:, :channels] = decoded_i[...].astype(F32)
    held[:, channels:] = to_slabs(grad_latent, crops, count)
    me = me_i[0, 0]
    part = held.shape[0] // count
    for k in range(count):
        backs[k][...] = bfloat(held[pl.ds(pl.multiple_of((me ^ k) * part, 8), part), :])
    post_grad = dot_tn(quant, grad_post)
    bias = jnp.concatenate([stacked([total(grad_post.astype(F32))])] * 2, axis=1)
    share, e_share = vectors_i.shape[1] // (2 * mine.shape[0]), embed // (2 * mine.shape[0])
    vectors[...] = jnp.concatenate([vectors_i[...], bias], axis=0)
    core = core_i[0, 0]
    for d in range(2 * mine.shape[0]):
        rows = jnp.concatenate(
            [vectors[:16, d * share : (d + 1) * share], vectors[16:, d * e_share : d * e_share + share]], axis=0
        )
        lines = mine.shape[1]
        left = post_grad[d * e_share : (d + 1) * e_share]
        if e_share < lines:
            left = jnp.concatenate([left, jnp.zeros((lines - e_share, embed), F32)], axis=0)
        if lines > 24:
            rows = jnp.concatenate([rows, jnp.zeros((lines - 24, share), F32)], axis=0)
        rows = jnp.concatenate([rows, jnp.zeros((lines, mine.shape[2] - embed - share), F32)], axis=1)
        block = bfloat(jnp.concatenate([left, rows], axis=1))

        @pl.when(core == d % 2)
        def _():
            mine[d // 2] = block

        @pl.when(core != d % 2)
        def _():
            other[d // 2] = block


def post_back(crops, count, width, chips, me, core, grad, masks, quant, post_w, vectors, decoded, afters, weight):
    rows, channels = grad.shape
    embed = quant.shape[1]
    out = ((chips, max(32, embed // (2 * chips)), channels), BF16)
    return call(
        functools.partial(post_kernel, crops, count, width),
        [(me, SMEM), (core, SMEM)]
        + [(a, VMEM) for a in (grad, masks, quant, post_w, vectors, decoded)]
        + [(a, ANY) for a in (*afters, weight)],
        [((rows // count, channels + embed), BF16)] * count + [out, out],
        [
            pltpu.VMEM(weight.shape, BF16),
            pltpu.VMEM((rows, 9 * channels), BF16),
            pltpu.VMEM((rows, channels + embed), F32),
            pltpu.VMEM((24, channels), F32),
            pltpu.SemaphoreType.DMA((1,)),
        ],
        5.6,
    )


def assemble_kernel(crops, count, me_i, *refs):
    pieces, (latent, decoded_o, latent_o) = refs[:count], (refs[count], *refs[-2:])
    channels = decoded_o.shape[3]
    lines, width = decoded_o.shape[1:3]
    me = me_i[0, 0]
    for k in range(count):
        piece = pieces[k][...].astype(F32)
        for c in range(crops):
            crop = (me ^ k) * crops + c
            for y in range(lines):
                line = piece[(c * lines + y) * width : (c * lines + y + 1) * width]
                decoded_o[crop, y] = bfloat(line[:, :channels])
                latent_o[crop, y] = line[:, channels:] + 2.0 * BETA_COMMIT * latent[crop, y].astype(F32)


def assemble(crops, me, pieces, latent, channels, afters):
    return call(
        functools.partial(assemble_kernel, crops, len(pieces)),
        [(me, SMEM)] + [(p, VMEM) for p in (*pieces, latent)] + [(a, ANY) for a in afters],
        [(latent.shape[:3] + (channels,), BF16), (latent.shape, F32)],
        [],
        0.1,
        SMALL,
    )


def weight_grad_kernel(width, together, afters, place_i, *refs):
    refs, (mine, other, columns, sums) = refs[: -4 - afters], refs[-4:]
    acts, *grads, masks = refs
    step = pl.program_id(0)
    count, rows, lanes = acts.shape
    core, chip = place_i[0, 0], place_i[0, 1]
    blocks = [acts[i] if together else acts[chip ^ i] for i in range(count)]
    act = jnp.transpose(jnp.concatenate([b.astype(F32) for b in blocks], axis=0), (1, 0))
    for tap in range(9):
        shift = (tap // 3 - 1) * width + tap % 3 - 1
        moved = act
        if shift:
            moved = pltpu.roll(act, (-shift) % (count * rows), 1) * masks[tap : tap + 1, :]
        columns[tap * lanes : (tap + 1) * lanes, :] = bfloat(moved)
    if together:
        grad = grads[0][...].reshape(count * rows, grads[0].shape[2])
    else:
        grad = jnp.concatenate([g[...] for g in grads], axis=0)
    part = dot(columns[...], grad)

    @pl.when(step == 0)
    def _():
        sums[...] = part

    @pl.when(step > 0)
    def _():
        sums[...] += part

    @pl.when(step == pl.num_programs(0) - 1)
    def _():
        share = mine.shape[1]
        for own in range(2):

            @pl.when(core == own)
            def _():
                for tap in range(9):
                    for out, half in ((mine, own), (other, 1 - own)):
                        start = tap * lanes + half * share
                        out[tap] = bfloat(sums[start : start + share])


def weight_grad(width, channels, here, acts, place, share, grads, masks, *afters, part=0):
    together = not isinstance(grads, (list, tuple))
    grads = [grads] if together else list(grads)
    count, rows, _ = acts.shape
    lanes = -(-2 * share // 128) * 128
    block = min(count, 4)
    out = jax.ShapeDtypeStruct((9, share, channels), BF16)
    if together:
        grad_specs = [pl.BlockSpec((block, rows, channels), lambda i: (i, part, 0))]
    else:
        grad_specs = [pl.BlockSpec((rows, channels), lambda i: (0, 0))] * count
    return pl.pallas_call(
        functools.partial(weight_grad_kernel, width, together, len(afters)),
        grid=(count // block,),
        in_specs=[SMEM, pl.BlockSpec((block, rows, lanes), lambda i: (i, 0, place))]
        + grad_specs
        + [pl.BlockSpec(masks.shape, lambda i: (0, 0))]
        + [ANY] * len(afters),
        out_specs=[pl.BlockSpec(out.shape, lambda i: (0, 0, 0))] * 2,
        out_shape=[out, out],
        scratch_shapes=[
            pltpu.VMEM((9 * lanes, block * rows), BF16),
            pltpu.VMEM((9 * lanes, channels), F32),
        ],
        cost_estimate=cost(1.0),
        compiler_params=pltpu.CompilerParams(vmem_limit_bytes=VMEM_BYTES),
    )(here, acts, *grads, masks, *afters)


def round_kernel(steps, parity_i, *refs):
    parity = parity_i[0, 0]
    for kind, inputs, outputs, scratch in steps:
        ins = [refs[i] for i in inputs]
        outs = [refs[i] for i in outputs]
        if kind == "add":
            outs[0][...] = bfloat(ins[0][...].astype(F32) + ins[1][...].astype(F32))
        elif kind == "sum":
            sums = ins[0][0].astype(F32)
            for i in range(1, ins[0].shape[0]):
                sums = sums + ins[0][i].astype(F32)
            outs[0][...] = sums
        elif kind == "join":
            both = [ref[...].astype(F32) for ref in ins]
            for own in range(2):

                @pl.when(parity == own)
                def _():
                    whole = jnp.concatenate([both[own], both[1 - own]], axis=0)
                    outs[0][...] = whole.reshape(outs[0].shape)

        else:
            parts = [ref[...] for ref in ins] if kind == "split" else [ins[0][i] for i in range(ins[0].shape[0])]
            sums = parts[0].astype(F32)
            for part in parts[1:]:
                sums = sums + part.astype(F32)
            held = refs[scratch]
            held[...] = sums.reshape(held.shape)
            outs[0][...] = held[parity]
            outs[1][...] = bfloat(held[1 - parity])


def step_round(parity, steps, afters=()):
    inputs, outputs, scratch, plan = [], [], [], []
    for kind, *args in steps:
        arrays = args[:2] if kind in ("add", "join", "split") else args
        ids = list(range(len(inputs), len(inputs) + len(arrays)))
        inputs += arrays
        lanes = arrays[0].shape[-1]
        if kind == "add":
            made = [(arrays[0].shape, BF16)]
        elif kind == "sum":
            made = [(arrays[0].shape[1:], F32)]
        elif kind == "join":
            made = [(args[2], F32)]
        else:
            rows = arrays[0].size // lanes // (arrays[0].shape[0] if kind == "blocks" else 1)
            made = [((rows // 2, lanes), F32), ((rows // 2, lanes), BF16)]
            scratch.append((2, rows // 2, lanes))
        plan.append((kind, ids, list(range(len(outputs), len(outputs) + len(made))), len(scratch) - 1))
        outputs += made
    first_out = len(inputs) + len(afters)
    first_scratch = first_out + len(outputs)
    plan = [(kind, ids, [first_out + o for o in outs], first_scratch + s) for kind, ids, outs, s in plan]
    return call(
        functools.partial(round_kernel, plan),
        [(parity, SMEM)] + [(a, VMEM) for a in inputs] + [(a, ANY) for a in afters],
        outputs,
        [pltpu.VMEM(s, F32) for s in scratch],
        0.1,
        SMALL,
    )


def to_crop_owners(tensor):
    return lax.all_to_all(tensor, "row", 0, 0, tiled=True)


def from_around(send):
    count = lax.axis_size("row")
    got = [lax.ppermute(send(k), "row", [(i, i ^ k) for i in range(count)]) for k in range(1, count)]
    return [send(0)] + got


def across_chips(tensor):
    count = lax.axis_size("dp")
    groups = [[2 * i + c for i in range(count // 2)] for c in range(2)]
    return lax.all_to_all(tensor, "dp", 0, 0, axis_index_groups=groups, tiled=True)


def from_sibling(other):
    return lax.ppermute(other, "dp", [(i, i ^ 1) for i in range(lax.axis_size("dp"))])


def from_sibling(other):
    return lax.ppermute(other, "dp", [(i, i ^ 1) for i in range(lax.axis_size("dp"))])


def from_all_chips(tensor):
    count = lax.axis_size("dp")
    chips = count // 2
    if chips in (1, 2, 4):
        return [tensor] + [
            lax.ppermute(tensor, "dp", [(i, i ^ (2 * k)) for i in range(count)]) for k in range(1, chips)
        ]
    return across_chips(jnp.broadcast_to(tensor[None], (chips,) + tensor.shape))


def swap_rows(tensor, step):
    return lax.ppermute(tensor, "row", [(i, i ^ step) for i in range(lax.axis_size("row"))])


def on_device(
    latent,
    codes,
    codebook,
    post_weight,
    post_bias,
    entry_weight,
    entry_bias,
    first_gain,
    first_shift,
    first_weight,
    first_bias,
    second_gain,
    second_shift,
    second_weight,
    second_bias,
    mixer_gain,
    mixer_shift,
    query_weight,
    query_bias,
    key_weight,
    value_weight,
    value_bias,
    projection_output_weight,
    projection_output_bias,
    cotangent,
):
    batch, rows_local, width, embed = latent.shape
    channels = entry_weight.shape[2]
    row_count = lax.axis_size("row")
    dp_count = lax.axis_size("dp")
    chips = dp_count // 2
    owned = codebook.shape[0]
    height = rows_local * row_count
    crops = batch // row_count
    sequence = height * width
    positions = crops * sequence
    me = lax.axis_index("row")
    dp = lax.axis_index("dp")
    here = jnp.stack([dp % 2, dp // 2]).astype(jnp.int32).reshape(1, 2)
    row_place = me.astype(jnp.int32).reshape(1, 1)
    parity = row_place % 2
    masks = tap_masks(crops, height, width)
    share, e_share = channels // dp_count, embed // dp_count

    code_row = codes.reshape(1, positions)
    all_codes = from_around(lambda k: code_row)
    found, *for_others = lookup(row_place, all_codes, codebook)
    pieces = from_around(lambda k: for_others[k])
    cot = to_crop_owners(cotangent.reshape(row_count, -1, channels)).reshape(positions, channels)
    quant, acts, normed, attended, decoded, standard_one, standard_two, standard_mix, inverses, query, key, value, probs = forward(
        crops,
        width,
        pieces,
        masks,
        post_weight,
        (post_bias, entry_bias, first_gain, first_shift, first_bias, second_gain, second_shift, second_bias, mixer_gain, mixer_shift, query_bias, value_bias, projection_output_bias),
        (entry_weight, first_weight, second_weight, query_weight, key_weight, value_weight, projection_output_weight),
        chips,
    )
    acts = across_chips(acts)
    cot, grad_q, grad_k, grad_v, grads_all, grad_stream, vectors = backward(
        crops,
        width,
        row_count,
        chips,
        (cot, masks, standard_one, standard_two, standard_mix, inverses, query, key, value, probs),
        (first_gain, first_shift, second_gain, second_shift, mixer_gain),
        quant,
        (projection_output_weight, query_weight, key_weight, value_weight, second_weight, first_weight),
    )
    grads_all = across_chips(grads_all)
    *backs, small_mine, small_other = post_back(
        crops, row_count, width, chips, row_place, here, grad_stream, masks, quant, post_weight, vectors, decoded, (acts,), entry_weight
    )
    latent_flat = late(latent.reshape(positions, embed), small_mine)
    latents = from_around(lambda k: latent_flat)
    joint_mine, joint_other = attention_grads(
        dp_count, here, (normed, attended, cot, grad_q, grad_k, grad_v, small_mine, small_other), (latent_flat,)
    )
    book_mine, book_other = scatter(
        row_place, here, all_codes, latents, found, codebook.shape[0], chips, (joint_mine,)
    )
    wide_masks = jnp.tile(masks.T, (1, min(chips, 4)))
    second_mine, second_other = weight_grad(
        width, channels, here, acts, 0, share, grads_all, wide_masks, book_mine
    )
    first_mine, first_other = weight_grad(
        width, channels, here, acts, 1, share, grads_all, wide_masks, second_mine, part=1
    )
    (joint,) = step_round(parity, [("add", joint_mine, from_sibling(joint_other))], (first_mine,))
    joint_all = across_chips(joint)
    keep_a, away_a = step_round(parity, [("split", second_mine, from_sibling(second_other))], (joint,))
    entry_mine, entry_other = weight_grad(
        width, channels, here, acts, 2, e_share, grads_all, wide_masks, away_a, part=2
    )
    keep_b, away_b = step_round(parity, [("split", first_mine, from_sibling(first_other))], (entry_mine,))
    keep_c, away_c = step_round(parity, [("split", entry_mine, from_sibling(entry_other))], (away_b,))
    (half_a,) = step_round(parity, [("add", keep_a, swap_rows(away_a, 1))], (away_c,))
    (book,) = step_round(parity, [("add", book_mine, from_sibling(book_other))], (half_a,))
    (half_b,) = step_round(parity, [("add", keep_b, swap_rows(away_b, 1))], (book,))
    half_c, keep_d, away_d = step_round(
        parity, [("add", keep_c, swap_rows(away_c, 1)), ("blocks", joint_all)], (half_b,)
    )
    book_all = across_chips(book)
    (half_a,) = step_round(parity, [("add", half_a, swap_rows(half_a, 2))], (half_c,))
    decoded, latent_grad = assemble(
        crops, row_place, from_around(lambda k: backs[k]), latent, channels, (half_a,)
    )
    (half_d,) = step_round(parity, [("add", keep_d, swap_rows(away_d, 1))], (decoded,))
    (half_b,) = step_round(parity, [("add", half_b, swap_rows(half_b, 2))], (half_d,))
    (second_w,) = step_round(parity, [("join", half_a, swap_rows(half_a, 1), (9, share, channels))], (half_b,))
    half_c, half_d = step_round(
        parity,
        [("add", half_c, swap_rows(half_c, 2)), ("add", half_d, swap_rows(half_d, 2))],
        (second_w,),
    )
    first_w, codebook_grad = step_round(
        parity,
        [("join", half_b, swap_rows(half_b, 1), (9, share, channels)), ("sum", book_all)],
        (half_d,),
    )
    entry_w, sum_d = step_round(
        parity,
        [
            ("join", half_c, swap_rows(half_c, 1), (9, e_share, channels)),
            ("join", half_d, swap_rows(half_d, 1), joint.shape[1:]),
        ],
        (first_w,),
    )

    o_w, q_w, k_w, v_w = (sum_d[i * share : (i + 1) * share] for i in range(4))
    small = sum_d[4 * share :]
    post_w = small[:e_share, :embed]
    vec = [small[i, embed : embed + share] for i in (0, 1, 2, 3, 4, 5, 8, 9, 10, 11, 12, 13)]
    post_b = small[16, embed : embed + e_share]
    gain_1, shift_1, b_entry, gain_2, shift_2, b_first, gain_m, shift_m, b_q, b_v, b_o, b_second = vec
    return (
        decoded,
        latent_grad,
        codebook_grad,
        post_w,
        post_b,
        entry_w,
        b_entry,
        gain_1,
        shift_1,
        first_w,
        b_first,
        gain_2,
        shift_2,
        second_w,
        b_second,
        gain_m,
        shift_m,
        q_w,
        b_q,
        k_w,
        v_w,
        b_v,
        o_w,
        b_o,
    )


def solution(mesh):
    def cells(depth):
        return P("dp", "row", *([None] * depth))

    return jax.shard_map(
        on_device,
        mesh=mesh,
        in_specs=(cells(2), cells(1), P("row", None)) + (P(),) * 21 + (cells(2),),
        out_specs=(
            cells(2),
            cells(2),
            P(("row", "dp"), None),
            P("dp", None),
            P("dp"),
            P(None, "dp", None),
            P("dp"),
            P("dp"),
            P("dp"),
            P(None, "dp", None),
            P("dp"),
            P("dp"),
            P("dp"),
            P(None, "dp", None),
            P("dp"),
            P("dp"),
            P("dp"),
            P("dp", None),
            P("dp"),
            P("dp", None),
            P("dp", None),
            P("dp"),
            P("dp", None),
            P("dp"),
        ),
        check_vma=False,
    )
```

```python
import functools

import jax
import jax.numpy as jnp
from jax import lax
from jax.experimental import pallas as pl
from jax.experimental.pallas import tpu as pltpu
from jax.sharding import PartitionSpec as P

GROUPS = 32
EPSILON = 1e-06
BETA_COMMIT = 0.25
F32 = jnp.float32
BF16 = jnp.bfloat16
SMALL = 4 * 1024 * 1024
MICROS = {
    "lookup": 5.4,
    "forward": 12,
    "backward": 11.0,
    "post": 5.6,
    "late": 0.1,
    "attention": 4.0,
    "scatter": 5.0,
    "assemble": 0.1,
    "weightsA": 4.5,
    "weightsB": 4.5,
    "weightsC": 8,
    "splitA": 2,
    "joint": 2,
    "nearA": 2,
    "splitB": 2,
    "book": 2,
    "splitC": 2,
    "nearB": 2,
    "farA": 2,
    "nearC-splitD": 2,
    "farB": 2,
    "wholeA": 2,
    "nearD": 2,
    "farC-farD": 2,
    "wholeB": 2,
    "wholeD-codes": 2,
    "wholeC": 2,
}
MEBIBYTES = {
    "lookup": 56,
    "forward": 56,
    "backward": 56,
    "post": 56,
    "attention": 56,
    "scatter": 56,
    "weightsA": 56,
    "weightsB": 56,
    "weightsC": 56,
}
ORDER = (
    ("post",),
    ("late",),
    ("attention",),
    ("scatter",),
    ("assemble",),
    ("weightsA",),
    ("weightsC",),
    ("weightsB",),
    ("splitA",),
    ("joint",),
    ("nearA",),
    ("splitB",),
    ("book",),
    ("splitC",),
    ("nearB",),
    ("farA",),
    ("nearC", "splitD",),
    ("farB",),
    ("wholeA",),
    ("nearD",),
    ("farC", "farD",),
    ("wholeB",),
    ("wholeD", "codes",),
    ("wholeC",),
)
VMEM = pl.BlockSpec(memory_space=pltpu.VMEM)
ANY = pl.BlockSpec(memory_space=pl.ANY)
SMEM = pl.BlockSpec(memory_space=pltpu.SMEM)


def bfloat(tensor):
    return tensor.astype(BF16)


def rounded(tensor):
    return lax.reduce_precision(tensor, 8, 7).astype(BF16)


def dot(a, b):
    return lax.dot_general(a, b, (((1,), (0,)), ((), ())), preferred_element_type=F32)


def dot_nt(a, b):
    return lax.dot_general(a, b, (((1,), (1,)), ((), ())), preferred_element_type=F32)


def dot_tn(a, b):
    return lax.dot_general(a, b, (((0,), (0,)), ((), ())), preferred_element_type=F32)


def same_group(channels):
    width = channels // GROUPS
    row = lax.broadcasted_iota(jnp.int32, (channels, channels), 0) // width
    col = lax.broadcasted_iota(jnp.int32, (channels, channels), 1) // width
    return (row == col).astype(F32).astype(BF16)


def stacked(rows):
    place = lax.broadcasted_iota(jnp.int32, (8, rows[0].shape[1]), 0)
    out = jnp.zeros((8, rows[0].shape[1]), F32)
    for i, row in enumerate(rows):
        out = jnp.where(place == i, row, out)
    return out


def group_sums(rows, group):
    high = bfloat(rows).astype(F32)
    rest = rows - high
    mid = bfloat(rest).astype(F32)
    parts = bfloat(jnp.concatenate([high, mid, rest - mid], axis=0))
    sums = dot(parts, group)
    return sums[0:8] + sums[8:16] + sums[16:24]


def by_crop(tensor, crops):
    size = tensor.shape[0] // crops
    return [tensor[i * size : (i + 1) * size] for i in range(crops)]


def total(tensor):
    return jnp.sum(tensor, axis=0, keepdims=True)


def norm(tensor, group, crops):
    parts = by_crop(tensor, crops)
    members = parts[0].shape[0] * (tensor.shape[1] // GROUPS)
    means = group_sums(stacked([total(p) for p in parts]), group) * (1.0 / members)
    parts = [p - means[i : i + 1] for i, p in enumerate(parts)]
    spread = group_sums(stacked([total(p * p) for p in parts]), group) * (1.0 / members)
    inverse = lax.rsqrt(spread + EPSILON)
    standard = jnp.concatenate([p * inverse[i : i + 1] for i, p in enumerate(parts)], axis=0)
    return standard, inverse


def norm_back(grad, standard, inverse, gain, group, crops):
    grads, normals = by_crop(grad, crops), by_crop(standard, crops)
    members = grads[0].shape[0] * (grad.shape[1] // GROUPS)
    firsts = [total(g) for g in grads]
    seconds = [total(g * n) for g, n in zip(grads, normals)]
    means = group_sums(stacked([v * gain for v in firsts + seconds]), group) * (1.0 / members)
    outs = [
        (g * gain - means[i : i + 1] - n * means[crops + i : crops + i + 1]) * inverse[i : i + 1]
        for i, (g, n) in enumerate(zip(grads, normals))
    ]
    return jnp.concatenate(outs, axis=0), sum(seconds[1:], seconds[0]), sum(firsts[1:], firsts[0])


def spread_taps(out_ref, tensor, mask_ref, width, sign):
    rows, lanes = tensor.shape
    for tap in range(9):
        step = sign * ((tap // 3 - 1) * width + tap % 3 - 1)
        moved = tensor
        if step:
            seen = tap if sign > 0 else 8 - tap
            moved = pltpu.roll(tensor, (-step) % rows, 0) * mask_ref[:, seen : seen + 1]
        out_ref[:, tap * lanes : (tap + 1) * lanes] = bfloat(moved)


def tap_masks(crops, height, width):
    y = jnp.arange(height).reshape(1, height, 1, 1)
    x = jnp.arange(width).reshape(1, 1, width, 1)
    tap = jnp.arange(16).reshape(1, 1, 1, 16)
    dy, dx = tap // 3 - 1, tap % 3 - 1
    fits = (y + dy >= 0) & (y + dy < height) & (x + dx >= 0) & (x + dx < width)
    return jnp.broadcast_to(fits, (crops, height, width, 16)).reshape(-1, 16).astype(F32)


def silu_slope(pre_act):
    logistic = jax.nn.sigmoid(pre_act)
    return logistic * (1.0 + pre_act * (1.0 - logistic))


def fetch(sources, buffers, sems):
    copies = [
        pltpu.make_async_copy(s, b, sems.at[i]) for i, (s, b) in enumerate(zip(sources, buffers))
    ]
    for copy in copies:
        copy.start()
    return copies


def cost(name):
    return pl.CostEstimate(flops=int(MICROS[name] * 1.15e9), bytes_accessed=0, transcendentals=0)


TOKEN = jax.ShapeDtypeStruct((8, 128), F32)


def call(kernel, inputs, outputs, scratch, name, token=None, limit=None):
    given, made = len(inputs), len(outputs)
    outputs = [jax.ShapeDtypeStruct(s, d) for s, d in outputs]

    def in_turn(*refs):
        refs[given + 1 + made][...] = jnp.zeros(TOKEN.shape, TOKEN.dtype)
        kernel(*refs[:given], *refs[given + 1 : given + 1 + made], *refs[given + 2 + made :])

    if token is not None:
        inputs, outputs = [*inputs, (token, ANY)], [*outputs, TOKEN]
    return pl.pallas_call(
        kernel if token is None else in_turn,
        out_shape=outputs,
        in_specs=[s for _, s in inputs],
        out_specs=[VMEM] * len(outputs),
        scratch_shapes=scratch,
        cost_estimate=cost(name),
        compiler_params=pltpu.CompilerParams(vmem_limit_bytes=limit or MEBIBYTES[name] * 2**20),
    )(*[a for a, _ in inputs])


def to_crops(tensor, crops, count):
    part = tensor.shape[0] // (crops * count)
    return jnp.concatenate(
        [tensor[(s * crops + c) * part : (s * crops + c + 1) * part] for c in range(crops) for s in range(count)], axis=0
    )


def to_slabs(tensor, crops, count):
    part = tensor.shape[0] // (crops * count)
    return jnp.concatenate(
        [tensor[(c * count + s) * part : (c * count + s + 1) * part] for s in range(count) for c in range(crops)], axis=0
    )


def put_blocks(out, place, tensor):
    chips, _, lanes = out.shape
    lanes //= 3
    share = tensor.shape[1] // chips
    for i in range(chips):
        block = tensor[:, i * share : (i + 1) * share]
        if share < lanes:
            block = jnp.concatenate([block, jnp.zeros((tensor.shape[0], lanes - share), block.dtype)], axis=1)
        out[i, :, place * lanes : (place + 1) * lanes] = block


def late_kernel(array, out):
    out[...] = array[...]


def late(array, token):
    return call(late_kernel, [(array, VMEM)], [(array.shape, array.dtype)], [], "late", token, SMALL)


def lookup_kernel(count, me_i, *refs):
    codes, book, found_o, refs = refs[:count], refs[count], refs[count + 1], refs[count + 2 :]
    outs, (one_hot, held) = refs[:count], refs[count:]
    owned = book.shape[0]
    size = codes[0].shape[1]
    me = me_i[0, 0]
    lane = lax.broadcasted_iota(jnp.int32, (size, 128), 1)
    for k in range(count):
        wanted = codes[k][...] - me * owned
        wanted = jnp.transpose(jnp.broadcast_to(wanted, (128, size)), (1, 0)) - lane
        for start in range(0, owned, 128):
            one_hot[k * size : (k + 1) * size, start : start + 128] = bfloat((wanted == start).astype(F32))
    found = dot(one_hot[...], book[...])
    held[...] = found
    found_o[...] = bfloat(found)
    part = size // count
    for k in range(count):
        rows = [
            held[pl.ds(pl.multiple_of((s ^ me) * size + (me ^ k) * part, 8), part), :] for s in range(count)
        ]
        outs[k][...] = bfloat(jnp.concatenate(rows, axis=0))


def lookup(me, codes, book):
    count, size, embed = len(codes), codes[0].shape[1], book.shape[1]
    return call(
        functools.partial(lookup_kernel, count),
        [(me, SMEM)] + [(c, VMEM) for c in codes] + [(book, VMEM)],
        [((count * size, embed), BF16)] + [((size, embed), BF16)] * count,
        [pltpu.VMEM((count * size, book.shape[0]), BF16), pltpu.VMEM((count * size, embed), F32)],
        "lookup",
    )


def scatter_kernel(count, me_i, *refs):
    codes, latents, found, core_i = refs[:count], refs[count : 2 * count], refs[2 * count], refs[2 * count + 1]
    mine, other, gaps, sums_s = refs[-4:]
    chips, rows, _ = mine.shape
    owned = 2 * chips * rows
    core = core_i[0, 0]
    size = codes[0].shape[1]
    me = me_i[0, 0]
    for k in range(count):
        latent = latents[k][...].astype(F32)
        here = slice(k * size, (k + 1) * size)
        gaps[here, :] = bfloat(2.0 * (found[here, :].astype(F32) - latent))
    block = max(2 * rows, 1024)
    row = lax.broadcasted_iota(jnp.int32, (block, size), 0)
    for start in range(0, owned, block):
        one_hot = [bfloat((row == codes[k][...] - (me * owned + start)).astype(F32)) for k in range(count)]
        sums = dot(one_hot[0], gaps[:size, :])
        for k in range(1, count):
            sums = sums + dot(one_hot[k], gaps[k * size : (k + 1) * size, :])
        sums_s[...] = sums
        for d in range(block // (2 * rows)):
            for out, half in ((mine, core), (other, 1 - core)):
                here = pl.ds(pl.multiple_of((2 * d + half) * rows, 8), rows)
                out[start // (2 * rows) + d] = bfloat(sums_s[here, :])


def scatter(me, core, codes, latents, found, owned, chips, token):
    count, size, embed = len(codes), codes[0].shape[1], found.shape[1]
    return call(
        functools.partial(scatter_kernel, count),
        [(me, SMEM)]
        + [(a, VMEM) for a in (*codes, *latents, found)]
        + [(core, SMEM)],
        [((chips, owned // (2 * chips), embed), BF16)] * 2,
        [
            pltpu.VMEM((count * size, embed), BF16),
            pltpu.VMEM((max(owned // chips, 1024), embed), F32),
        ],
        "scatter",
        token,
    )


def forward_kernel(crops, width, count, *refs):
    pieces, refs = refs[:count], refs[count:]
    (
        masks, post_w, vectors, *refs,
    ) = refs
    entry_b, gain_1, shift_1, bias_1, gain_2, shift_2, bias_2, gain_m, shift_m, q_b, v_b, o_b = (
        vectors.at[i : i + 1] for i in range(12)
    )
    post_b = vectors.at[12:13, : post_w.shape[1]]
    sources, refs = refs[:7], refs[7:]
    (
        quant_o, acts_o, normed_o, attended_o, decoded_o, standard_1, standard_2, standard_m, inverses,
        query_o, key_o, value_o, probs_o, *refs,
    ) = refs
    entry_w, first_w, second_w, q_w, k_w, v_w, o_w, columns, hidden_s, sems = refs
    copies = fetch(sources, refs[:7], sems)
    channels = entry_w.shape[1]
    rows = quant_o.shape[0]
    size = rows // crops
    scale = channels ** (-0.5)
    found = pieces[0][...].astype(F32)
    for piece in pieces[1:]:
        found = found + piece[...].astype(F32)
    quant = bfloat(to_crops(found, crops, count))
    quant_o[...] = quant
    post = bfloat(dot(quant, post_w[...]) + post_b[...])
    put_blocks(acts_o, 2, post)
    embed = post.shape[1]
    spread_taps(columns.at[:, : 9 * embed], post.astype(F32), masks, width, 1)
    group = same_group(channels)
    copies[0].wait()
    stream = dot(columns[:, : 9 * embed], entry_w[...]) + entry_b[...]
    hidden_s[...] = stream
    standard, inverse = norm(stream, group, crops)
    standard_1[...] = standard
    inverses[0] = inverse
    act = bfloat(jax.nn.silu(standard * gain_1[...] + shift_1[...]))
    put_blocks(acts_o, 1, act)
    spread_taps(columns, act.astype(F32), masks, width, 1)
    copies[1].wait()
    middle = dot(columns[...], first_w[...].reshape(9 * channels, channels)) + bias_1[...]
    standard, inverse = norm(middle, group, crops)
    standard_2[...] = standard
    inverses[1] = inverse
    act = bfloat(jax.nn.silu(standard * gain_2[...] + shift_2[...]))
    put_blocks(acts_o, 0, act)
    spread_taps(columns, act.astype(F32), masks, width, 1)
    copies[2].wait()
    hidden = hidden_s[...] + (dot(columns[...], second_w[...].reshape(9 * channels, channels)) + bias_2[...])
    hidden_s[...] = hidden
    standard, inverse = norm(hidden, group, crops)
    standard_m[...] = standard
    inverses[2] = inverse
    normed = bfloat(standard * gain_m[...] + shift_m[...])
    normed_o[...] = normed
    for copy in copies[3:]:
        copy.wait()
    query_o[...] = bfloat(dot(normed, q_w[...]) + q_b[...])
    key_o[...] = bfloat(dot(normed, k_w[...]))
    value_o[...] = bfloat(dot(normed, v_w[...]) + v_b[...])
    for i in range(crops):
        here = slice(i * size, (i + 1) * size)
        logits = dot_nt(query_o[here, :], key_o[here, :]) * scale
        exponents = jnp.exp(logits - jnp.max(logits, axis=1, keepdims=True))
        probs = exponents / jnp.sum(exponents, axis=1, keepdims=True)
        probs_o[i] = probs
        attended_o[here, :] = bfloat(dot(bfloat(probs), value_o[here, :]))
    result = bfloat(dot(attended_o[...], o_w[...]) + o_b[...])
    decoded_o[...] = bfloat(to_slabs(hidden_s[...] + result.astype(F32), crops, count))


def forward(crops, width, pieces, masks, post_w, vectors, weights, chips, token):
    rows, embed = pieces[0].shape
    channels = weights[0].shape[2]
    wide = (rows, channels)
    lanes = 3 * (-(-channels // chips // 128) * 128)
    buffers = [w.reshape(-1, channels) if w.shape[1] == embed else w for w in weights]
    return call(
        functools.partial(forward_kernel, crops, width, len(pieces)),
        [(a, VMEM) for a in (*pieces, masks, post_w, vectors)] + [(w, ANY) for w in buffers],
        [((rows, embed), BF16), ((chips, rows, lanes), BF16)]
        + [(wide, BF16)] * 3
        + [(wide, F32)] * 3
        + [((3, 8, channels), F32)]
        + [(wide, BF16)] * 3
        + [((crops, rows // crops, rows // crops), F32)],
        [pltpu.VMEM(w.shape, BF16) for w in buffers]
        + [
            pltpu.VMEM((rows, 9 * channels), BF16),
            pltpu.VMEM(wide, F32),
            pltpu.SemaphoreType.DMA((len(buffers),)),
        ],
        "forward",
        token,
    )


def backward_kernel(crops, width, count, *refs):
    (
        cot_i, masks, standard_1, standard_2, standard_m, inverses, query, key, value, probs_i, vectors_i, *refs,
    ) = refs
    gain_1, shift_1, gain_2, shift_2, gain_m = (vectors_i.at[i : i + 1] for i in (1, 2, 4, 5, 7))
    sources, refs = refs[:6], refs[6:]
    cot_o, grad_q_o, grad_k_o, grad_v_o, all_o, stream_o, vectors_o, *refs = refs
    o_w, q_w, k_w, v_w, second_w, first_w, columns, hidden_s, sems = refs
    copies = fetch(sources, refs[:6], sems)
    rows, channels = query.shape
    size = rows // crops
    scale = channels ** (-0.5)
    group = same_group(channels)
    cot = bfloat(to_crops(cot_i[...].astype(F32), crops, count))
    cot_o[...] = cot
    copies[0].wait()
    grads_att = by_crop(bfloat(dot_nt(cot, o_w[...])), crops)
    for i in range(crops):
        here = slice(i * size, (i + 1) * size)
        grad_att, probs = grads_att[i], probs_i[i]
        grad_w = dot_nt(grad_att, value[here, :])
        grad_v_o[here, :] = bfloat(dot_tn(bfloat(probs), grad_att))
        grad_s = bfloat(probs * (grad_w - jnp.sum(grad_w * probs, axis=1, keepdims=True)))
        grad_q_o[here, :] = bfloat(dot(grad_s, key[here, :]) * scale)
        grad_k_o[here, :] = bfloat(dot_tn(grad_s, query[here, :]) * scale)
    grad_q, grad_k, grad_v = grad_q_o[...], grad_k_o[...], grad_v_o[...]
    for copy in copies[1:4]:
        copy.wait()
    grad_normed = bfloat(dot_nt(grad_q, q_w[...]) + dot_nt(grad_k, k_w[...]) + dot_nt(grad_v, v_w[...]))
    grad, gain_grad_m, shift_grad_m = norm_back(
        grad_normed.astype(F32), standard_m[...], inverses[2], gain_m[...], group, crops
    )
    grad = cot.astype(F32) + grad
    hidden_s[...] = grad
    branch = bfloat(grad)

    def through(grad, weight, standard_ref, inverse, gain_ref, shift_ref):
        grad = conv_back(grad, masks, width, weight, columns)
        standard, gain = standard_ref[...], gain_ref[...]
        grad = grad * silu_slope(standard * gain + shift_ref[...])
        return norm_back(grad, standard, inverse, gain, group, crops)

    copies[4].wait()
    grad, gain_grad_2, shift_grad_2 = through(branch, second_w, standard_2, inverses[1], gain_2, shift_2)
    middle = bfloat(grad)
    copies[5].wait()
    grad, gain_grad_1, shift_grad_1 = through(middle, first_w, standard_1, inverses[0], gain_1, shift_1)
    stream = bfloat(hidden_s[...] + grad)
    stream_o[...] = stream
    for i in range(all_o.shape[0]):
        all_o[i, :rows] = branch
        all_o[i, rows : 2 * rows] = middle
        all_o[i, 2 * rows :] = stream
    sums = [total(v.astype(F32)) for v in (stream, middle, grad_q, grad_v, cot, branch)]
    vectors_o[0:8] = stacked([gain_grad_1, shift_grad_1, sums[0], gain_grad_2, shift_grad_2, sums[1]])
    vectors_o[8:16] = stacked([gain_grad_m, shift_grad_m, *sums[2:]])


def backward(crops, width, count, chips, arrays, vectors, weights):
    rows, channels = arrays[0].shape
    wide = (rows, channels)
    return call(
        functools.partial(backward_kernel, crops, width, count),
        [(a, VMEM) for a in (*arrays, vectors)] + [(w, ANY) for w in weights],
        [(wide, BF16)] * 4
        + [((chips, 3 * rows, channels), BF16), (wide, BF16), ((16, channels), F32)],
        [pltpu.VMEM(w.shape, BF16) for w in weights]
        + [
            pltpu.VMEM((rows, 9 * channels), BF16),
            pltpu.VMEM(wide, F32),
            pltpu.SemaphoreType.DMA((len(weights),)),
        ],
        "backward",
    )


def attention_grads_kernel(core_i, normed, attended, cot, grad_q, grad_k, grad_v, small_mine, small_other, *refs):
    mine, other, wide = refs[-3:]
    core = core_i[0, 0]
    channels = normed.shape[1]
    pairs = ((attended, cot), (normed, grad_q), (normed, grad_k), (normed, grad_v))
    share = (mine.shape[1] - small_mine.shape[1]) // len(pairs)
    mine[:, len(pairs) * share :] = small_mine[...]
    other[:, len(pairs) * share :] = small_other[...]
    for i, (a, b) in enumerate(pairs):
        wide[...] = dot_tn(a[...], b[...])
        for d in range(channels // (2 * share)):
            for out, half in ((mine, core), (other, 1 - core)):
                start = pl.multiple_of((2 * d + half) * share, 8)
                out[d, i * share : (i + 1) * share, :] = bfloat(wide[pl.ds(start, share), :])


def attention_grads(dp_count, core, arrays, token):
    rows, channels = arrays[0].shape
    share = channels // dp_count
    out = ((dp_count // 2, 4 * share + arrays[-1].shape[1], channels), BF16)
    return call(
        attention_grads_kernel,
        [(core, SMEM)] + [(a, VMEM) for a in arrays],
        [out, out],
        [pltpu.VMEM((channels, channels), F32)],
        "attention",
        token,
    )


def conv_back(grad, masks, width, weight, columns):
    lanes = grad.shape[1]
    spread_taps(columns, grad.astype(F32), masks, width, -1)
    out = dot_nt(columns[:, :lanes], weight[0])
    for tap in range(1, 9):
        out = out + dot_nt(columns[:, tap * lanes : (tap + 1) * lanes], weight[tap])
    return out


def post_kernel(
    crops, count, width, me_i, core_i, grad_i, masks, quant_i, post_w, vectors_i, decoded_i, *refs,
):
    weight_hbm, *refs = refs[-count - 8 :]
    backs, (mine, other, weight, columns, held, vectors, sems) = refs[:count], refs[count:]
    copies = fetch((weight_hbm,), (weight,), sems)
    copies[0].wait()
    grad_post = bfloat(conv_back(grad_i[...], masks, width, weight, columns))
    quant = quant_i[...]
    embed = quant.shape[1]
    grad_latent = dot_nt(grad_post, post_w[...]) - 2.0 * BETA_COMMIT * quant.astype(F32)
    channels = decoded_i.shape[1]
    held[:, :channels] = decoded_i[...].astype(F32)
    held[:, channels:] = to_slabs(grad_latent, crops, count)
    me = me_i[0, 0]
    part = held.shape[0] // count
    for k in range(count):
        backs[k][...] = bfloat(held[pl.ds(pl.multiple_of((me ^ k) * part, 8), part), :])
    post_grad = dot_tn(quant, grad_post)
    bias = jnp.concatenate([stacked([total(grad_post.astype(F32))])] * 2, axis=1)
    share, e_share = vectors_i.shape[1] // (2 * mine.shape[0]), embed // (2 * mine.shape[0])
    vectors[...] = jnp.concatenate([vectors_i[...], bias], axis=0)
    core = core_i[0, 0]
    for d in range(2 * mine.shape[0]):
        rows = jnp.concatenate(
            [vectors[:16, d * share : (d + 1) * share], vectors[16:, d * e_share : d * e_share + share]], axis=0
        )
        lines = mine.shape[1]
        left = post_grad[d * e_share : (d + 1) * e_share]
        if e_share < lines:
            left = jnp.concatenate([left, jnp.zeros((lines - e_share, embed), F32)], axis=0)
        if lines > 24:
            rows = jnp.concatenate([rows, jnp.zeros((lines - 24, share), F32)], axis=0)
        rows = jnp.concatenate([rows, jnp.zeros((lines, mine.shape[2] - embed - share), F32)], axis=1)
        block = bfloat(jnp.concatenate([left, rows], axis=1))

        @pl.when(core == d % 2)
        def _():
            mine[d // 2] = block

        @pl.when(core != d % 2)
        def _():
            other[d // 2] = block


def post_back(crops, count, width, chips, me, core, grad, masks, quant, post_w, vectors, decoded, token, weight):
    rows, channels = grad.shape
    embed = quant.shape[1]
    out = ((chips, max(32, embed // (2 * chips)), channels), BF16)
    return call(
        functools.partial(post_kernel, crops, count, width),
        [(me, SMEM), (core, SMEM)]
        + [(a, VMEM) for a in (grad, masks, quant, post_w, vectors, decoded)]
        + [(weight, ANY)],
        [((rows // count, channels + embed), BF16)] * count + [out, out],
        [
            pltpu.VMEM(weight.shape, BF16),
            pltpu.VMEM((rows, 9 * channels), BF16),
            pltpu.VMEM((rows, channels + embed), F32),
            pltpu.VMEM((24, channels), F32),
            pltpu.SemaphoreType.DMA((1,)),
        ],
        "post",
        token,
    )


def assemble_kernel(crops, count, me_i, *refs):
    pieces, (latent, decoded_o, latent_o) = refs[:count], (refs[count], *refs[-2:])
    channels = decoded_o.shape[3]
    lines, width = decoded_o.shape[1:3]
    me = me_i[0, 0]
    for k in range(count):
        piece = pieces[k][...].astype(F32)
        for c in range(crops):
            crop = (me ^ k) * crops + c
            for y in range(lines):
                line = piece[(c * lines + y) * width : (c * lines + y + 1) * width]
                decoded_o[crop, y] = bfloat(line[:, :channels])
                latent_o[crop, y] = line[:, channels:] + 2.0 * BETA_COMMIT * latent[crop, y].astype(F32)


def assemble(crops, me, pieces, latent, channels, token):
    return call(
        functools.partial(assemble_kernel, crops, len(pieces)),
        [(me, SMEM)] + [(p, VMEM) for p in (*pieces, latent)],
        [(latent.shape[:3] + (channels,), BF16), (latent.shape, F32)],
        [],
        "assemble",
        token,
        SMALL,
    )


def weight_grad_kernel(width, place_i, acts, grads, masks, _, mine, other, token, columns, sums):
    token[...] = jnp.zeros(token.shape, token.dtype)
    step = pl.program_id(0)
    count, rows, lanes = acts.shape
    core = place_i[0, 0]
    act = jnp.transpose(acts[...].reshape(count * rows, lanes).astype(F32), (1, 0))
    for tap in range(9):
        shift = (tap // 3 - 1) * width + tap % 3 - 1
        moved = act
        if shift:
            moved = pltpu.roll(act, (-shift) % (count * rows), 1) * masks[tap : tap + 1, :]
        columns[tap * lanes : (tap + 1) * lanes, :] = bfloat(moved)
    part = dot(columns[...], grads[...].reshape(count * rows, grads.shape[2]))

    @pl.when(step == 0)
    def _():
        sums[...] = part

    @pl.when(step > 0)
    def _():
        sums[...] += part

    @pl.when(step == pl.num_programs(0) - 1)
    def _():
        share = mine.shape[1]
        for own in range(2):

            @pl.when(core == own)
            def _():
                for tap in range(9):
                    for out, half in ((mine, own), (other, 1 - own)):
                        start = tap * lanes + half * share
                        out[tap] = bfloat(sums[start : start + share])


def weight_grad(name, width, channels, here, acts, place, share, grads, masks, token, part=0):
    count, rows, _ = acts.shape
    lanes = -(-2 * share // 128) * 128
    block = min(count, 4)
    out = jax.ShapeDtypeStruct((9, share, channels), BF16)
    return pl.pallas_call(
        functools.partial(weight_grad_kernel, width),
        grid=(count // block,),
        in_specs=[
            SMEM,
            pl.BlockSpec((block, rows, lanes), lambda i: (i, 0, place)),
            pl.BlockSpec((block, rows, channels), lambda i: (i, part, 0)),
            pl.BlockSpec(masks.shape, lambda i: (0, 0)),
            ANY,
        ],
        out_specs=[pl.BlockSpec(out.shape, lambda i: (0, 0, 0))] * 2 + [pl.BlockSpec(TOKEN.shape, lambda i: (0, 0))],
        out_shape=[out, out, TOKEN],
        scratch_shapes=[
            pltpu.VMEM((9 * lanes, block * rows), BF16),
            pltpu.VMEM((9 * lanes, channels), F32),
        ],
        cost_estimate=cost(name),
        compiler_params=pltpu.CompilerParams(vmem_limit_bytes=MEBIBYTES[name] * 2**20),
    )(here, acts, grads, masks, token)


def round_kernel(steps, parity_i, *refs):
    parity = parity_i[0, 0]
    for kind, inputs, outputs, scratch in steps:
        ins = [refs[i] for i in inputs]
        outs = [refs[i] for i in outputs]
        if kind == "add":
            outs[0][...] = bfloat(ins[0][...].astype(F32) + ins[1][...].astype(F32))
        elif kind == "sum":
            sums = ins[0][0].astype(F32)
            for i in range(1, ins[0].shape[0]):
                sums = sums + ins[0][i].astype(F32)
            outs[0][...] = sums
        elif kind == "join":
            both = [ref[...].astype(F32) for ref in ins]
            for own in range(2):

                @pl.when(parity == own)
                def _():
                    whole = jnp.concatenate([both[own], both[1 - own]], axis=0)
                    outs[0][...] = whole.reshape(outs[0].shape)

        else:
            parts = [ref[...] for ref in ins] if kind == "split" else [ins[0][i] for i in range(ins[0].shape[0])]
            sums = parts[0].astype(F32)
            for part in parts[1:]:
                sums = sums + part.astype(F32)
            held = refs[scratch]
            held[...] = sums.reshape(held.shape)
            outs[0][...] = held[parity]
            outs[1][...] = bfloat(held[1 - parity])


def step_round(name, parity, steps, token):
    inputs, outputs, scratch, plan = [], [], [], []
    for kind, *args in steps:
        arrays = args[:2] if kind in ("add", "join", "split") else args
        ids = list(range(len(inputs), len(inputs) + len(arrays)))
        inputs += arrays
        lanes = arrays[0].shape[-1]
        if kind == "add":
            made = [(arrays[0].shape, BF16)]
        elif kind == "sum":
            made = [(arrays[0].shape[1:], F32)]
        elif kind == "join":
            made = [(args[2], F32)]
        else:
            rows = arrays[0].size // lanes // (arrays[0].shape[0] if kind == "blocks" else 1)
            made = [((rows // 2, lanes), F32), ((rows // 2, lanes), BF16)]
            scratch.append((2, rows // 2, lanes))
        plan.append((kind, ids, list(range(len(outputs), len(outputs) + len(made))), len(scratch) - 1))
        outputs += made
    first_out = len(inputs)
    first_scratch = first_out + len(outputs)
    plan = [(kind, ids, [first_out + o for o in outs], first_scratch + s) for kind, ids, outs, s in plan]
    return call(
        functools.partial(round_kernel, plan),
        [(parity, SMEM)] + [(a, VMEM) for a in inputs],
        outputs,
        [pltpu.VMEM(s, F32) for s in scratch],
        name,
        token,
        SMALL,
    )


def to_crop_owners(tensor):
    return lax.all_to_all(tensor, "row", 0, 0, tiled=True)


def from_around(send):
    count = lax.axis_size("row")
    got = [lax.ppermute(send(k), "row", [(i, i ^ k) for i in range(count)]) for k in range(1, count)]
    return [send(0)] + got


def across_chips(tensor):
    count = lax.axis_size("dp")
    groups = [[2 * i + c for i in range(count // 2)] for c in range(2)]
    return lax.all_to_all(tensor, "dp", 0, 0, axis_index_groups=groups, tiled=True)


def from_sibling(other):
    return lax.ppermute(other, "dp", [(i, i ^ 1) for i in range(lax.axis_size("dp"))])


def from_sibling(other):
    return lax.ppermute(other, "dp", [(i, i ^ 1) for i in range(lax.axis_size("dp"))])


def from_all_chips(tensor):
    count = lax.axis_size("dp")
    chips = count // 2
    if chips in (1, 2, 4):
        return [tensor] + [
            lax.ppermute(tensor, "dp", [(i, i ^ (2 * k)) for i in range(count)]) for k in range(1, chips)
        ]
    return across_chips(jnp.broadcast_to(tensor[None], (chips,) + tensor.shape))


def swap_rows(tensor, step):
    return lax.ppermute(tensor, "row", [(i, i ^ step) for i in range(lax.axis_size("row"))])


def on_device(
    latent,
    codes,
    codebook,
    post_weight,
    post_bias,
    entry_weight,
    entry_bias,
    first_gain,
    first_shift,
    first_weight,
    first_bias,
    second_gain,
    second_shift,
    second_weight,
    second_bias,
    mixer_gain,
    mixer_shift,
    query_weight,
    query_bias,
    key_weight,
    value_weight,
    value_bias,
    projection_output_weight,
    projection_output_bias,
    cotangent,
):
    batch, rows_local, width, embed = latent.shape
    channels = entry_weight.shape[2]
    row_count = lax.axis_size("row")
    dp_count = lax.axis_size("dp")
    chips = dp_count // 2
    owned = codebook.shape[0]
    height = rows_local * row_count
    crops = batch // row_count
    sequence = height * width
    positions = crops * sequence
    me = lax.axis_index("row")
    dp = lax.axis_index("dp")
    here = jnp.stack([dp % 2, dp // 2]).astype(jnp.int32).reshape(1, 2)
    row_place = me.astype(jnp.int32).reshape(1, 1)
    parity = row_place % 2
    masks = tap_masks(crops, height, width)
    share, e_share = channels // dp_count, embed // dp_count

    small_params = jnp.stack(
        [entry_bias, first_gain, first_shift, first_bias, second_gain, second_shift, second_bias, mixer_gain, mixer_shift, query_bias, value_bias, projection_output_bias]
        + [jnp.pad(post_bias, (0, channels - embed))]
        + [jnp.zeros_like(entry_bias)] * 3
    )

    code_row = codes.reshape(1, positions)
    all_codes = from_around(lambda k: code_row)
    found, *for_others = lookup(row_place, all_codes, codebook)
    pieces = from_around(lambda k: for_others[k])
    cot_late, cot_token = late(cotangent.reshape(row_count, -1, channels), pieces[1])
    cot = to_crop_owners(cot_late).reshape(positions, channels)
    quant, acts, normed, attended, decoded, standard_one, standard_two, standard_mix, inverses, query, key, value, probs, _ = forward(
        crops,
        width,
        pieces,
        masks,
        post_weight,
        small_params,
        (entry_weight, first_weight, second_weight, query_weight, key_weight, value_weight, projection_output_weight),
        chips,
        cot_token,
    )
    acts = across_chips(acts)
    cot, grad_q, grad_k, grad_v, grads_all, grad_stream, vectors = backward(
        crops,
        width,
        row_count,
        chips,
        (cot, masks, standard_one, standard_two, standard_mix, inverses, query, key, value, probs),
        small_params,
        (projection_output_weight, query_weight, key_weight, value_weight, second_weight, first_weight),
    )
    grads_all = across_chips(grads_all)
    wide_masks = jnp.tile(masks.T, (1, min(chips, 4)))
    latent_flat = latent.reshape(positions, embed)
    made = {}

    def sums_step(task):
        kind, of = task[:-1], task[-1]
        if task == "joint":
            return ("add", made["joint_mine"], from_sibling(made["joint_other"])), ["joint"]
        if task == "book":
            return ("add", made["book_mine"], from_sibling(made["book_other"])), ["book"]
        if task == "codes":
            return ("sum", across_chips(made["book"])), ["codebook_grad"]
        if task == "splitD":
            return ("blocks", across_chips(made["joint"])), ["keepD", "awayD"]
        if kind == "split":
            return ("split", made["mine" + of], from_sibling(made["other" + of])), ["keep" + of, "away" + of]
        if kind == "near":
            return ("add", made["keep" + of], swap_rows(made["away" + of], 1)), ["near" + of]
        if kind == "far":
            return ("add", made["near" + of], swap_rows(made["near" + of], 2)), ["far" + of]
        shape = {"A": (9, share, channels), "B": (9, share, channels), "C": (9, e_share, channels)}
        shape = shape.get(of, made["joint"].shape[1:])
        return ("join", made["far" + of], swap_rows(made["far" + of], 1), shape), ["whole" + of]

    token = vectors
    weights = {"A": (0, share), "B": (1, share), "C": (2, e_share)}
    for group in ORDER:
        task = group[0]
        if task == "post":
            *backs, small_mine, small_other, token = post_back(
                crops, row_count, width, chips, row_place, here, grad_stream, masks, quant, post_weight, vectors, decoded, token, entry_weight
            )
        elif task == "late":
            latent_late, token = late(latent_flat, token)
            latents = from_around(lambda k: latent_late)
        elif task == "attention":
            made["joint_mine"], made["joint_other"], token = attention_grads(
                dp_count, here, (normed, attended, cot, grad_q, grad_k, grad_v, small_mine, small_other), token
            )
        elif task == "scatter":
            made["book_mine"], made["book_other"], token = scatter(
                row_place, here, all_codes, latents, found, codebook.shape[0], chips, token
            )
        elif task == "assemble":
            decoded, latent_grad, token = assemble(
                crops, row_place, from_around(lambda k: backs[k]), latent, channels, token
            )
        elif task[:-1] == "weights":
            place, rows = weights[task[-1]]
            made["mine" + task[-1]], made["other" + task[-1]], token = weight_grad(
                task, width, channels, here, acts, place, rows, grads_all, wide_masks, token, part=place
            )
        else:
            steps, names = zip(*(sums_step(t) for t in group))
            *results, token = step_round("-".join(group), parity, list(steps), token)
            made.update(zip(sum(names, []), results))
    second_w, first_w, entry_w, sum_d, codebook_grad = (
        made[name] for name in ("wholeA", "wholeB", "wholeC", "wholeD", "codebook_grad")
    )

    o_w, q_w, k_w, v_w = (sum_d[i * share : (i + 1) * share] for i in range(4))
    small = sum_d[4 * share :]
    post_w = small[:e_share, :embed]
    vec = [small[i, embed : embed + share] for i in (0, 1, 2, 3, 4, 5, 8, 9, 10, 11, 12, 13)]
    post_b = small[16, embed : embed + e_share]
    gain_1, shift_1, b_entry, gain_2, shift_2, b_first, gain_m, shift_m, b_q, b_v, b_o, b_second = vec
    return (
        decoded,
        latent_grad,
        codebook_grad,
        post_w,
        post_b,
        entry_w,
        b_entry,
        gain_1,
        shift_1,
        first_w,
        b_first,
        gain_2,
        shift_2,
        second_w,
        b_second,
        gain_m,
        shift_m,
        q_w,
        b_q,
        k_w,
        v_w,
        b_v,
        o_w,
        b_o,
    )


def solution(mesh):
    def cells(depth):
        return P("dp", "row", *([None] * depth))

    return jax.shard_map(
        on_device,
        mesh=mesh,
        in_specs=(cells(2), cells(1), P("row", None)) + (P(),) * 21 + (cells(2),),
        out_specs=(
            cells(2),
            cells(2),
            P(("row", "dp"), None),
            P("dp", None),
            P("dp"),
            P(None, "dp", None),
            P("dp"),
            P("dp"),
            P("dp"),
            P(None, "dp", None),
            P("dp"),
            P("dp"),
            P("dp"),
            P(None, "dp", None),
            P("dp"),
            P("dp"),
            P("dp"),
            P("dp", None),
            P("dp"),
            P("dp", None),
            P("dp", None),
            P("dp"),
            P("dp", None),
            P("dp"),
        ),
        check_vma=False,
    )
```

```python
import functools

import jax
import jax.numpy as jnp
from jax import lax
from jax.experimental import pallas as pl
from jax.experimental.pallas import tpu as pltpu
from jax.sharding import PartitionSpec as P

GROUPS = 32
EPSILON = 1e-06
BETA_COMMIT = 0.25
F32 = jnp.float32
BF16 = jnp.bfloat16
SMALL = 4 * 1024 * 1024
MICROS = {
    "lookup": 5.4,
    "forward": 12,
    "backward": 11.0,
    "post": 5.6,
    "late": 0.1,
    "attention": 4.0,
    "scatter": 5.0,
    "assemble": 0.1,
    "weightsA": 4.5,
    "weightsB": 4.5,
    "weightsC": 8,
    "splitA": 2,
    "joint": 2,
    "splitB": 2,
    "nearA": 2,
    "book": 2,
    "splitC": 2,
    "nearB": 2,
    "farA": 2,
    "nearC-splitD": 2,
    "farB": 2,
    "wholeA": 2,
    "nearD": 2,
    "farC-farD": 2,
    "wholeB": 2,
    "wholeD-codes": 2,
    "wholeC": 2,
}
MEBIBYTES = {
    "lookup": 24,
    "forward": 56,
    "backward": 56,
    "post": 56,
    "attention": 56,
    "scatter": 56,
    "weightsA": 56,
    "weightsB": 56,
    "weightsC": 56,
}
ORDER = (
    ("post",),
    ("late",),
    ("attention",),
    ("scatter",),
    ("assemble",),
    ("weightsA",),
    ("weightsC",),
    ("weightsB",),
    ("splitA",),
    ("joint",),
    ("splitB",),
    ("nearA",),
    ("book",),
    ("splitC",),
    ("nearB",),
    ("farA",),
    ("nearC", "splitD",),
    ("farB",),
    ("wholeA",),
    ("nearD",),
    ("farC", "farD",),
    ("wholeB",),
    ("wholeD", "codes",),
    ("wholeC",),
)
VMEM = pl.BlockSpec(memory_space=pltpu.VMEM)
ANY = pl.BlockSpec(memory_space=pl.ANY)
SMEM = pl.BlockSpec(memory_space=pltpu.SMEM)


def bfloat(tensor):
    return tensor.astype(BF16)


def rounded(tensor):
    return lax.reduce_precision(tensor, 8, 7).astype(BF16)


def dot(a, b):
    return lax.dot_general(a, b, (((1,), (0,)), ((), ())), preferred_element_type=F32)


def dot_nt(a, b):
    return lax.dot_general(a, b, (((1,), (1,)), ((), ())), preferred_element_type=F32)


def dot_tn(a, b):
    return lax.dot_general(a, b, (((0,), (0,)), ((), ())), preferred_element_type=F32)


def same_group(channels):
    width = channels // GROUPS
    row = lax.broadcasted_iota(jnp.int32, (channels, channels), 0) // width
    col = lax.broadcasted_iota(jnp.int32, (channels, channels), 1) // width
    return (row == col).astype(F32).astype(BF16)


def stacked(rows):
    place = lax.broadcasted_iota(jnp.int32, (8, rows[0].shape[1]), 0)
    out = jnp.zeros((8, rows[0].shape[1]), F32)
    for i, row in enumerate(rows):
        out = jnp.where(place == i, row, out)
    return out


def group_sums(rows, group):
    high = bfloat(rows).astype(F32)
    rest = rows - high
    mid = bfloat(rest).astype(F32)
    parts = bfloat(jnp.concatenate([high, mid, rest - mid], axis=0))
    sums = dot(parts, group)
    return sums[0:8] + sums[8:16] + sums[16:24]


def by_crop(tensor, crops):
    size = tensor.shape[0] // crops
    return [tensor[i * size : (i + 1) * size] for i in range(crops)]


def total(tensor):
    return jnp.sum(tensor, axis=0, keepdims=True)


def norm(tensor, group, crops):
    parts = by_crop(tensor, crops)
    members = parts[0].shape[0] * (tensor.shape[1] // GROUPS)
    means = group_sums(stacked([total(p) for p in parts]), group) * (1.0 / members)
    parts = [p - means[i : i + 1] for i, p in enumerate(parts)]
    spread = group_sums(stacked([total(p * p) for p in parts]), group) * (1.0 / members)
    inverse = lax.rsqrt(spread + EPSILON)
    standard = jnp.concatenate([p * inverse[i : i + 1] for i, p in enumerate(parts)], axis=0)
    return standard, inverse


def norm_back(grad, standard, inverse, gain, group, crops):
    grads, normals = by_crop(grad, crops), by_crop(standard, crops)
    members = grads[0].shape[0] * (grad.shape[1] // GROUPS)
    firsts = [total(g) for g in grads]
    seconds = [total(g * n) for g, n in zip(grads, normals)]
    means = group_sums(stacked([v * gain for v in firsts + seconds]), group) * (1.0 / members)
    outs = [
        (g * gain - means[i : i + 1] - n * means[crops + i : crops + i + 1]) * inverse[i : i + 1]
        for i, (g, n) in enumerate(zip(grads, normals))
    ]
    return jnp.concatenate(outs, axis=0), sum(seconds[1:], seconds[0]), sum(firsts[1:], firsts[0])


def spread_taps(out_ref, tensor, mask_ref, width, sign):
    rows, lanes = tensor.shape
    for tap in range(9):
        step = sign * ((tap // 3 - 1) * width + tap % 3 - 1)
        moved = tensor
        if step:
            seen = tap if sign > 0 else 8 - tap
            moved = pltpu.roll(tensor, (-step) % rows, 0) * mask_ref[:, seen : seen + 1]
        out_ref[:, tap * lanes : (tap + 1) * lanes] = bfloat(moved)


def tap_masks(crops, height, width):
    y = jnp.arange(height).reshape(1, height, 1, 1)
    x = jnp.arange(width).reshape(1, 1, width, 1)
    tap = jnp.arange(16).reshape(1, 1, 1, 16)
    dy, dx = tap // 3 - 1, tap % 3 - 1
    fits = (y + dy >= 0) & (y + dy < height) & (x + dx >= 0) & (x + dx < width)
    return jnp.broadcast_to(fits, (crops, height, width, 16)).reshape(-1, 16).astype(F32)


def silu_slope(pre_act):
    logistic = jax.nn.sigmoid(pre_act)
    return logistic * (1.0 + pre_act * (1.0 - logistic))


def fetch(sources, buffers, sems):
    copies = [
        pltpu.make_async_copy(s, b, sems.at[i]) for i, (s, b) in enumerate(zip(sources, buffers))
    ]
    for copy in copies:
        copy.start()
    return copies


def cost(name):
    return pl.CostEstimate(flops=int(MICROS[name] * 1.15e9), bytes_accessed=0, transcendentals=0)


TOKEN = jax.ShapeDtypeStruct((8, 128), F32)


def call(kernel, inputs, outputs, scratch, name, token=None, limit=None):
    given, made = len(inputs), len(outputs)
    outputs = [jax.ShapeDtypeStruct(s, d) for s, d in outputs]

    def in_turn(*refs):
        refs[given + 1 + made][...] = jnp.zeros(TOKEN.shape, TOKEN.dtype)
        kernel(*refs[:given], *refs[given + 1 : given + 1 + made], *refs[given + 2 + made :])

    if token is not None:
        inputs, outputs = [*inputs, (token, ANY)], [*outputs, TOKEN]
    return pl.pallas_call(
        kernel if token is None else in_turn,
        out_shape=outputs,
        in_specs=[s for _, s in inputs],
        out_specs=[VMEM] * len(outputs),
        scratch_shapes=scratch,
        cost_estimate=cost(name),
        compiler_params=pltpu.CompilerParams(vmem_limit_bytes=limit or MEBIBYTES[name] * 2**20),
    )(*[a for a, _ in inputs])


def to_crops(tensor, crops, count):
    part = tensor.shape[0] // (crops * count)
    return jnp.concatenate(
        [tensor[(s * crops + c) * part : (s * crops + c + 1) * part] for c in range(crops) for s in range(count)], axis=0
    )


def to_slabs(tensor, crops, count):
    part = tensor.shape[0] // (crops * count)
    return jnp.concatenate(
        [tensor[(c * count + s) * part : (c * count + s + 1) * part] for s in range(count) for c in range(crops)], axis=0
    )


def put_blocks(out, place, tensor):
    chips, _, lanes = out.shape
    lanes //= 3
    share = tensor.shape[1] // chips
    for i in range(chips):
        block = tensor[:, i * share : (i + 1) * share]
        if share < lanes:
            block = jnp.concatenate([block, jnp.zeros((tensor.shape[0], lanes - share), block.dtype)], axis=1)
        out[i, :, place * lanes : (place + 1) * lanes] = block


def late_kernel(array, out):
    out[...] = array[...]


def late(array, token):
    return call(late_kernel, [(array, VMEM)], [(array.shape, array.dtype)], [], "late", token, SMALL)


def lookup_kernel(count, me_i, *refs):
    codes, book, found_o, refs = refs[:count], refs[count], refs[count + 1], refs[count + 2 :]
    outs, (one_hot, held) = refs[:count], refs[count:]
    owned = book.shape[0]
    size = codes[0].shape[1]
    me = me_i[0, 0]
    lane = lax.broadcasted_iota(jnp.int32, (size, 128), 1)
    for k in range(count):
        wanted = codes[k][...] - me * owned
        wanted = jnp.transpose(jnp.broadcast_to(wanted, (128, size)), (1, 0)) - lane
        for start in range(0, owned, 128):
            one_hot[k * size : (k + 1) * size, start : start + 128] = bfloat((wanted == start).astype(F32))
    found = dot(one_hot[...], book[...])
    held[...] = found
    found_o[...] = bfloat(found)
    part = size // count
    for k in range(count):
        rows = [
            held[pl.ds(pl.multiple_of((s ^ me) * size + (me ^ k) * part, 8), part), :] for s in range(count)
        ]
        outs[k][...] = bfloat(jnp.concatenate(rows, axis=0))


def lookup(me, codes, book):
    count, size, embed = len(codes), codes[0].shape[1], book.shape[1]
    return call(
        functools.partial(lookup_kernel, count),
        [(me, SMEM)] + [(c, VMEM) for c in codes] + [(book, VMEM)],
        [((count * size, embed), BF16)] + [((size, embed), BF16)] * count,
        [pltpu.VMEM((count * size, book.shape[0]), BF16), pltpu.VMEM((count * size, embed), F32)],
        "lookup",
    )


def scatter_kernel(count, me_i, *refs):
    codes, latents, found, core_i = refs[:count], refs[count : 2 * count], refs[2 * count], refs[2 * count + 1]
    mine, other, gaps, sums_s = refs[-4:]
    chips, rows, _ = mine.shape
    owned = 2 * chips * rows
    core = core_i[0, 0]
    size = codes[0].shape[1]
    me = me_i[0, 0]
    for k in range(count):
        latent = latents[k][...].astype(F32)
        here = slice(k * size, (k + 1) * size)
        gaps[here, :] = bfloat(2.0 * (found[here, :].astype(F32) - latent))
    block = max(2 * rows, 1024)
    row = lax.broadcasted_iota(jnp.int32, (block, size), 0)
    for start in range(0, owned, block):
        one_hot = [bfloat((row == codes[k][...] - (me * owned + start)).astype(F32)) for k in range(count)]
        sums = dot(one_hot[0], gaps[:size, :])
        for k in range(1, count):
            sums = sums + dot(one_hot[k], gaps[k * size : (k + 1) * size, :])
        sums_s[...] = sums
        for d in range(block // (2 * rows)):
            for out, half in ((mine, core), (other, 1 - core)):
                here = pl.ds(pl.multiple_of((2 * d + half) * rows, 8), rows)
                out[start // (2 * rows) + d] = bfloat(sums_s[here, :])


def scatter(me, core, codes, latents, found, owned, chips, token):
    count, size, embed = len(codes), codes[0].shape[1], found.shape[1]
    return call(
        functools.partial(scatter_kernel, count),
        [(me, SMEM)]
        + [(a, VMEM) for a in (*codes, *latents, found)]
        + [(core, SMEM)],
        [((chips, owned // (2 * chips), embed), BF16)] * 2,
        [
            pltpu.VMEM((count * size, embed), BF16),
            pltpu.VMEM((max(owned // chips, 1024), embed), F32),
        ],
        "scatter",
        token,
    )


def forward_kernel(crops, width, count, *refs):
    pieces, refs = refs[:count], refs[count:]
    (
        masks, post_w, vectors, *refs,
    ) = refs
    entry_b, gain_1, shift_1, bias_1, gain_2, shift_2, bias_2, gain_m, shift_m, q_b, v_b, o_b = (
        vectors.at[i : i + 1] for i in range(12)
    )
    post_b = vectors.at[12:13, : post_w.shape[1]]
    sources, refs = refs[:7], refs[7:]
    (
        quant_o, acts_o, normed_o, attended_o, decoded_o, standard_1, standard_2, standard_m, inverses,
        query_o, key_o, value_o, probs_o, *refs,
    ) = refs
    entry_w, first_w, second_w, q_w, k_w, v_w, o_w, columns, hidden_s, sems = refs
    copies = fetch(sources, refs[:7], sems)
    channels = entry_w.shape[1]
    rows = quant_o.shape[0]
    size = rows // crops
    scale = channels ** (-0.5)
    found = pieces[0][...].astype(F32)
    for piece in pieces[1:]:
        found = found + piece[...].astype(F32)
    quant = bfloat(to_crops(found, crops, count))
    quant_o[...] = quant
    post = bfloat(dot(quant, post_w[...]) + post_b[...])
    put_blocks(acts_o, 2, post)
    embed = post.shape[1]
    spread_taps(columns.at[:, : 9 * embed], post.astype(F32), masks, width, 1)
    group = same_group(channels)
    copies[0].wait()
    stream = dot(columns[:, : 9 * embed], entry_w[...]) + entry_b[...]
    hidden_s[...] = stream
    standard, inverse = norm(stream, group, crops)
    standard_1[...] = standard
    inverses[0] = inverse
    act = bfloat(jax.nn.silu(standard * gain_1[...] + shift_1[...]))
    put_blocks(acts_o, 1, act)
    spread_taps(columns, act.astype(F32), masks, width, 1)
    copies[1].wait()
    middle = dot(columns[...], first_w[...].reshape(9 * channels, channels)) + bias_1[...]
    standard, inverse = norm(middle, group, crops)
    standard_2[...] = standard
    inverses[1] = inverse
    act = bfloat(jax.nn.silu(standard * gain_2[...] + shift_2[...]))
    put_blocks(acts_o, 0, act)
    spread_taps(columns, act.astype(F32), masks, width, 1)
    copies[2].wait()
    hidden = hidden_s[...] + (dot(columns[...], second_w[...].reshape(9 * channels, channels)) + bias_2[...])
    hidden_s[...] = hidden
    standard, inverse = norm(hidden, group, crops)
    standard_m[...] = standard
    inverses[2] = inverse
    normed = bfloat(standard * gain_m[...] + shift_m[...])
    normed_o[...] = normed
    for copy in copies[3:]:
        copy.wait()
    query_o[...] = bfloat(dot(normed, q_w[...]) + q_b[...])
    key_o[...] = bfloat(dot(normed, k_w[...]))
    value_o[...] = bfloat(dot(normed, v_w[...]) + v_b[...])
    for i in range(crops):
        here = slice(i * size, (i + 1) * size)
        logits = dot_nt(query_o[here, :], key_o[here, :]) * scale
        exponents = jnp.exp(logits - jnp.max(logits, axis=1, keepdims=True))
        probs = exponents / jnp.sum(exponents, axis=1, keepdims=True)
        probs_o[i] = probs
        attended_o[here, :] = bfloat(dot(bfloat(probs), value_o[here, :]))
    result = bfloat(dot(attended_o[...], o_w[...]) + o_b[...])
    decoded_o[...] = bfloat(to_slabs(hidden_s[...] + result.astype(F32), crops, count))


def forward(crops, width, pieces, masks, post_w, vectors, weights, chips, token):
    rows, embed = pieces[0].shape
    channels = weights[0].shape[2]
    wide = (rows, channels)
    lanes = 3 * (-(-channels // chips // 128) * 128)
    buffers = [w.reshape(-1, channels) if w.shape[1] == embed else w for w in weights]
    return call(
        functools.partial(forward_kernel, crops, width, len(pieces)),
        [(a, VMEM) for a in (*pieces, masks, post_w, vectors)] + [(w, ANY) for w in buffers],
        [((rows, embed), BF16), ((chips, rows, lanes), BF16)]
        + [(wide, BF16)] * 3
        + [(wide, F32)] * 3
        + [((3, 8, channels), F32)]
        + [(wide, BF16)] * 3
        + [((crops, rows // crops, rows // crops), F32)],
        [pltpu.VMEM(w.shape, BF16) for w in buffers]
        + [
            pltpu.VMEM((rows, 9 * channels), BF16),
            pltpu.VMEM(wide, F32),
            pltpu.SemaphoreType.DMA((len(buffers),)),
        ],
        "forward",
        token,
    )


def backward_kernel(crops, width, count, *refs):
    (
        cot_i, masks, standard_1, standard_2, standard_m, inverses, query, key, value, probs_i, vectors_i, *refs,
    ) = refs
    gain_1, shift_1, gain_2, shift_2, gain_m = (vectors_i.at[i : i + 1] for i in (1, 2, 4, 5, 7))
    sources, refs = refs[:6], refs[6:]
    cot_o, grad_q_o, grad_k_o, grad_v_o, all_o, stream_o, vectors_o, *refs = refs
    o_w, q_w, k_w, v_w, second_w, first_w, columns, hidden_s, sems = refs
    copies = fetch(sources, refs[:6], sems)
    rows, channels = query.shape
    size = rows // crops
    scale = channels ** (-0.5)
    group = same_group(channels)
    cot = bfloat(to_crops(cot_i[...].astype(F32), crops, count))
    cot_o[...] = cot
    copies[0].wait()
    grads_att = by_crop(bfloat(dot_nt(cot, o_w[...])), crops)
    for i in range(crops):
        here = slice(i * size, (i + 1) * size)
        grad_att, probs = grads_att[i], probs_i[i]
        grad_w = dot_nt(grad_att, value[here, :])
        grad_v_o[here, :] = bfloat(dot_tn(bfloat(probs), grad_att))
        grad_s = bfloat(probs * (grad_w - jnp.sum(grad_w * probs, axis=1, keepdims=True)))
        grad_q_o[here, :] = bfloat(dot(grad_s, key[here, :]) * scale)
        grad_k_o[here, :] = bfloat(dot_tn(grad_s, query[here, :]) * scale)
    grad_q, grad_k, grad_v = grad_q_o[...], grad_k_o[...], grad_v_o[...]
    for copy in copies[1:4]:
        copy.wait()
    grad_normed = bfloat(dot_nt(grad_q, q_w[...]) + dot_nt(grad_k, k_w[...]) + dot_nt(grad_v, v_w[...]))
    grad, gain_grad_m, shift_grad_m = norm_back(
        grad_normed.astype(F32), standard_m[...], inverses[2], gain_m[...], group, crops
    )
    grad = cot.astype(F32) + grad
    hidden_s[...] = grad
    branch = bfloat(grad)

    def through(grad, weight, standard_ref, inverse, gain_ref, shift_ref):
        grad = conv_back(grad, masks, width, weight, columns)
        standard, gain = standard_ref[...], gain_ref[...]
        grad = grad * silu_slope(standard * gain + shift_ref[...])
        return norm_back(grad, standard, inverse, gain, group, crops)

    copies[4].wait()
    grad, gain_grad_2, shift_grad_2 = through(branch, second_w, standard_2, inverses[1], gain_2, shift_2)
    middle = bfloat(grad)
    copies[5].wait()
    grad, gain_grad_1, shift_grad_1 = through(middle, first_w, standard_1, inverses[0], gain_1, shift_1)
    stream = bfloat(hidden_s[...] + grad)
    stream_o[...] = stream
    for i in range(all_o.shape[0]):
        all_o[i, :rows] = branch
        all_o[i, rows : 2 * rows] = middle
        all_o[i, 2 * rows :] = stream
    sums = [total(v.astype(F32)) for v in (stream, middle, grad_q, grad_v, cot, branch)]
    vectors_o[0:8] = stacked([gain_grad_1, shift_grad_1, sums[0], gain_grad_2, shift_grad_2, sums[1]])
    vectors_o[8:16] = stacked([gain_grad_m, shift_grad_m, *sums[2:]])


def backward(crops, width, count, chips, arrays, vectors, weights):
    rows, channels = arrays[0].shape
    wide = (rows, channels)
    return call(
        functools.partial(backward_kernel, crops, width, count),
        [(a, VMEM) for a in (*arrays, vectors)] + [(w, ANY) for w in weights],
        [(wide, BF16)] * 4
        + [((chips, 3 * rows, channels), BF16), (wide, BF16), ((16, channels), F32)],
        [pltpu.VMEM(w.shape, BF16) for w in weights]
        + [
            pltpu.VMEM((rows, 9 * channels), BF16),
            pltpu.VMEM(wide, F32),
            pltpu.SemaphoreType.DMA((len(weights),)),
        ],
        "backward",
    )


def attention_grads_kernel(core_i, normed, attended, cot, grad_q, grad_k, grad_v, small_mine, small_other, *refs):
    mine, other, wide = refs[-3:]
    core = core_i[0, 0]
    channels = normed.shape[1]
    pairs = ((attended, cot), (normed, grad_q), (normed, grad_k), (normed, grad_v))
    share = (mine.shape[1] - small_mine.shape[1]) // len(pairs)
    mine[:, len(pairs) * share :] = small_mine[...]
    other[:, len(pairs) * share :] = small_other[...]
    for i, (a, b) in enumerate(pairs):
        wide[...] = dot_tn(a[...], b[...])
        for d in range(channels // (2 * share)):
            for out, half in ((mine, core), (other, 1 - core)):
                start = pl.multiple_of((2 * d + half) * share, 8)
                out[d, i * share : (i + 1) * share, :] = bfloat(wide[pl.ds(start, share), :])


def attention_grads(dp_count, core, arrays, token):
    rows, channels = arrays[0].shape
    share = channels // dp_count
    out = ((dp_count // 2, 4 * share + arrays[-1].shape[1], channels), BF16)
    return call(
        attention_grads_kernel,
        [(core, SMEM)] + [(a, VMEM) for a in arrays],
        [out, out],
        [pltpu.VMEM((channels, channels), F32)],
        "attention",
        token,
    )


def conv_back(grad, masks, width, weight, columns):
    lanes = grad.shape[1]
    spread_taps(columns, grad.astype(F32), masks, width, -1)
    out = dot_nt(columns[:, :lanes], weight[0])
    for tap in range(1, 9):
        out = out + dot_nt(columns[:, tap * lanes : (tap + 1) * lanes], weight[tap])
    return out


def post_kernel(
    crops, count, width, me_i, core_i, grad_i, masks, quant_i, post_w, vectors_i, decoded_i, *refs,
):
    weight_hbm, *refs = refs[-count - 8 :]
    backs, (mine, other, weight, columns, held, vectors, sems) = refs[:count], refs[count:]
    copies = fetch((weight_hbm,), (weight,), sems)
    copies[0].wait()
    grad_post = bfloat(conv_back(grad_i[...], masks, width, weight, columns))
    quant = quant_i[...]
    embed = quant.shape[1]
    grad_latent = dot_nt(grad_post, post_w[...]) - 2.0 * BETA_COMMIT * quant.astype(F32)
    channels = decoded_i.shape[1]
    held[:, :channels] = decoded_i[...].astype(F32)
    held[:, channels:] = to_slabs(grad_latent, crops, count)
    me = me_i[0, 0]
    part = held.shape[0] // count
    for k in range(count):
        backs[k][...] = bfloat(held[pl.ds(pl.multiple_of((me ^ k) * part, 8), part), :])
    post_grad = dot_tn(quant, grad_post)
    bias = jnp.concatenate([stacked([total(grad_post.astype(F32))])] * 2, axis=1)
    share, e_share = vectors_i.shape[1] // (2 * mine.shape[0]), embed // (2 * mine.shape[0])
    vectors[...] = jnp.concatenate([vectors_i[...], bias], axis=0)
    core = core_i[0, 0]
    for d in range(2 * mine.shape[0]):
        rows = jnp.concatenate(
            [vectors[:16, d * share : (d + 1) * share], vectors[16:, d * e_share : d * e_share + share]], axis=0
        )
        lines = mine.shape[1]
        left = post_grad[d * e_share : (d + 1) * e_share]
        if e_share < lines:
            left = jnp.concatenate([left, jnp.zeros((lines - e_share, embed), F32)], axis=0)
        if lines > 24:
            rows = jnp.concatenate([rows, jnp.zeros((lines - 24, share), F32)], axis=0)
        rows = jnp.concatenate([rows, jnp.zeros((lines, mine.shape[2] - embed - share), F32)], axis=1)
        block = bfloat(jnp.concatenate([left, rows], axis=1))

        @pl.when(core == d % 2)
        def _():
            mine[d // 2] = block

        @pl.when(core != d % 2)
        def _():
            other[d // 2] = block


def post_back(crops, count, width, chips, me, core, grad, masks, quant, post_w, vectors, decoded, token, weight):
    rows, channels = grad.shape
    embed = quant.shape[1]
    out = ((chips, max(32, embed // (2 * chips)), channels), BF16)
    return call(
        functools.partial(post_kernel, crops, count, width),
        [(me, SMEM), (core, SMEM)]
        + [(a, VMEM) for a in (grad, masks, quant, post_w, vectors, decoded)]
        + [(weight, ANY)],
        [((rows // count, channels + embed), BF16)] * count + [out, out],
        [
            pltpu.VMEM(weight.shape, BF16),
            pltpu.VMEM((rows, 9 * channels), BF16),
            pltpu.VMEM((rows, channels + embed), F32),
            pltpu.VMEM((24, channels), F32),
            pltpu.SemaphoreType.DMA((1,)),
        ],
        "post",
        token,
    )


def assemble_kernel(crops, count, me_i, *refs):
    pieces, (latent, decoded_o, latent_o) = refs[:count], (refs[count], *refs[-2:])
    channels = decoded_o.shape[3]
    lines, width = decoded_o.shape[1:3]
    me = me_i[0, 0]
    for k in range(count):
        piece = pieces[k][...].astype(F32)
        for c in range(crops):
            crop = (me ^ k) * crops + c
            for y in range(lines):
                line = piece[(c * lines + y) * width : (c * lines + y + 1) * width]
                decoded_o[crop, y] = bfloat(line[:, :channels])
                latent_o[crop, y] = line[:, channels:] + 2.0 * BETA_COMMIT * latent[crop, y].astype(F32)


def assemble(crops, me, pieces, latent, channels, token):
    return call(
        functools.partial(assemble_kernel, crops, len(pieces)),
        [(me, SMEM)] + [(p, VMEM) for p in (*pieces, latent)],
        [(latent.shape[:3] + (channels,), BF16), (latent.shape, F32)],
        [],
        "assemble",
        token,
        SMALL,
    )


def weight_grad_kernel(width, place_i, acts, grads, masks, _, mine, other, token, columns, sums):
    token[...] = jnp.zeros(token.shape, token.dtype)
    step = pl.program_id(0)
    count, rows, lanes = acts.shape
    core = place_i[0, 0]
    act = jnp.transpose(acts[...].reshape(count * rows, lanes).astype(F32), (1, 0))
    for tap in range(9):
        shift = (tap // 3 - 1) * width + tap % 3 - 1
        moved = act
        if shift:
            moved = pltpu.roll(act, (-shift) % (count * rows), 1) * masks[tap : tap + 1, :]
        columns[tap * lanes : (tap + 1) * lanes, :] = bfloat(moved)
    part = dot(columns[...], grads[...].reshape(count * rows, grads.shape[2]))

    @pl.when(step == 0)
    def _():
        sums[...] = part

    @pl.when(step > 0)
    def _():
        sums[...] += part

    @pl.when(step == pl.num_programs(0) - 1)
    def _():
        share = mine.shape[1]
        for own in range(2):

            @pl.when(core == own)
            def _():
                for tap in range(9):
                    for out, half in ((mine, own), (other, 1 - own)):
                        start = tap * lanes + half * share
                        out[tap] = bfloat(sums[start : start + share])


def weight_grad(name, width, channels, here, acts, place, share, grads, masks, token, part=0):
    count, rows, _ = acts.shape
    lanes = -(-2 * share // 128) * 128
    block = min(count, 4)
    out = jax.ShapeDtypeStruct((9, share, channels), BF16)
    return pl.pallas_call(
        functools.partial(weight_grad_kernel, width),
        grid=(count // block,),
        in_specs=[
            SMEM,
            pl.BlockSpec((block, rows, lanes), lambda i: (i, 0, place)),
            pl.BlockSpec((block, rows, channels), lambda i: (i, part, 0)),
            pl.BlockSpec(masks.shape, lambda i: (0, 0)),
            ANY,
        ],
        out_specs=[pl.BlockSpec(out.shape, lambda i: (0, 0, 0))] * 2 + [pl.BlockSpec(TOKEN.shape, lambda i: (0, 0))],
        out_shape=[out, out, TOKEN],
        scratch_shapes=[
            pltpu.VMEM((9 * lanes, block * rows), BF16),
            pltpu.VMEM((9 * lanes, channels), F32),
        ],
        cost_estimate=cost(name),
        compiler_params=pltpu.CompilerParams(vmem_limit_bytes=MEBIBYTES[name] * 2**20),
    )(here, acts, grads, masks, token)


def round_kernel(steps, parity_i, *refs):
    parity = parity_i[0, 0]
    for kind, inputs, outputs, scratch in steps:
        ins = [refs[i] for i in inputs]
        outs = [refs[i] for i in outputs]
        if kind == "add":
            outs[0][...] = bfloat(ins[0][...].astype(F32) + ins[1][...].astype(F32))
        elif kind == "sum":
            sums = ins[0][0].astype(F32)
            for i in range(1, ins[0].shape[0]):
                sums = sums + ins[0][i].astype(F32)
            outs[0][...] = sums
        elif kind == "join":
            both = [ref[...].astype(F32) for ref in ins]
            for own in range(2):

                @pl.when(parity == own)
                def _():
                    whole = jnp.concatenate([both[own], both[1 - own]], axis=0)
                    outs[0][...] = whole.reshape(outs[0].shape)

        else:
            parts = [ref[...] for ref in ins] if kind == "split" else [ins[0][i] for i in range(ins[0].shape[0])]
            sums = parts[0].astype(F32)
            for part in parts[1:]:
                sums = sums + part.astype(F32)
            held = refs[scratch]
            held[...] = sums.reshape(held.shape)
            outs[0][...] = held[parity]
            outs[1][...] = bfloat(held[1 - parity])


def step_round(name, parity, steps, token):
    inputs, outputs, scratch, plan = [], [], [], []
    for kind, *args in steps:
        arrays = args[:2] if kind in ("add", "join", "split") else args
        ids = list(range(len(inputs), len(inputs) + len(arrays)))
        inputs += arrays
        lanes = arrays[0].shape[-1]
        if kind == "add":
            made = [(arrays[0].shape, BF16)]
        elif kind == "sum":
            made = [(arrays[0].shape[1:], F32)]
        elif kind == "join":
            made = [(args[2], F32)]
        else:
            rows = arrays[0].size // lanes // (arrays[0].shape[0] if kind == "blocks" else 1)
            made = [((rows // 2, lanes), F32), ((rows // 2, lanes), BF16)]
            scratch.append((2, rows // 2, lanes))
        plan.append((kind, ids, list(range(len(outputs), len(outputs) + len(made))), len(scratch) - 1))
        outputs += made
    first_out = len(inputs)
    first_scratch = first_out + len(outputs)
    plan = [(kind, ids, [first_out + o for o in outs], first_scratch + s) for kind, ids, outs, s in plan]
    return call(
        functools.partial(round_kernel, plan),
        [(parity, SMEM)] + [(a, VMEM) for a in inputs],
        outputs,
        [pltpu.VMEM(s, F32) for s in scratch],
        name,
        token,
        SMALL,
    )


def to_crop_owners(tensor):
    return lax.all_to_all(tensor, "row", 0, 0, tiled=True)


def from_around(send):
    count = lax.axis_size("row")
    got = [lax.ppermute(send(k), "row", [(i, i ^ k) for i in range(count)]) for k in range(1, count)]
    return [send(0)] + got


def across_chips(tensor):
    count = lax.axis_size("dp")
    groups = [[2 * i + c for i in range(count // 2)] for c in range(2)]
    return lax.all_to_all(tensor, "dp", 0, 0, axis_index_groups=groups, tiled=True)


def from_sibling(other):
    return lax.ppermute(other, "dp", [(i, i ^ 1) for i in range(lax.axis_size("dp"))])


def from_sibling(other):
    return lax.ppermute(other, "dp", [(i, i ^ 1) for i in range(lax.axis_size("dp"))])


def from_all_chips(tensor):
    count = lax.axis_size("dp")
    chips = count // 2
    if chips in (1, 2, 4):
        return [tensor] + [
            lax.ppermute(tensor, "dp", [(i, i ^ (2 * k)) for i in range(count)]) for k in range(1, chips)
        ]
    return across_chips(jnp.broadcast_to(tensor[None], (chips,) + tensor.shape))


def swap_rows(tensor, step):
    return lax.ppermute(tensor, "row", [(i, i ^ step) for i in range(lax.axis_size("row"))])


def on_device(
    latent,
    codes,
    codebook,
    post_weight,
    post_bias,
    entry_weight,
    entry_bias,
    first_gain,
    first_shift,
    first_weight,
    first_bias,
    second_gain,
    second_shift,
    second_weight,
    second_bias,
    mixer_gain,
    mixer_shift,
    query_weight,
    query_bias,
    key_weight,
    value_weight,
    value_bias,
    projection_output_weight,
    projection_output_bias,
    cotangent,
):
    batch, rows_local, width, embed = latent.shape
    channels = entry_weight.shape[2]
    row_count = lax.axis_size("row")
    dp_count = lax.axis_size("dp")
    chips = dp_count // 2
    owned = codebook.shape[0]
    height = rows_local * row_count
    crops = batch // row_count
    sequence = height * width
    positions = crops * sequence
    me = lax.axis_index("row")
    dp = lax.axis_index("dp")
    here = jnp.stack([dp % 2, dp // 2]).astype(jnp.int32).reshape(1, 2)
    row_place = me.astype(jnp.int32).reshape(1, 1)
    parity = row_place % 2
    masks = tap_masks(crops, height, width)
    share, e_share = channels // dp_count, embed // dp_count

    small_params = jnp.stack(
        [entry_bias, first_gain, first_shift, first_bias, second_gain, second_shift, second_bias, mixer_gain, mixer_shift, query_bias, value_bias, projection_output_bias]
        + [jnp.pad(post_bias, (0, channels - embed))]
        + [jnp.zeros_like(entry_bias)] * 3
    )

    code_row = codes.reshape(1, positions)
    all_codes = from_around(lambda k: code_row)
    found, *for_others = lookup(row_place, all_codes, codebook)
    pieces = from_around(lambda k: for_others[k])
    cot_late, cot_token = late(cotangent.reshape(row_count, -1, channels), pieces[1])
    cot = to_crop_owners(cot_late).reshape(positions, channels)
    quant, acts, normed, attended, decoded, standard_one, standard_two, standard_mix, inverses, query, key, value, probs, _ = forward(
        crops,
        width,
        pieces,
        masks,
        post_weight,
        small_params,
        (entry_weight, first_weight, second_weight, query_weight, key_weight, value_weight, projection_output_weight),
        chips,
        cot_token,
    )
    acts = across_chips(acts)
    cot, grad_q, grad_k, grad_v, grads_all, grad_stream, vectors = backward(
        crops,
        width,
        row_count,
        chips,
        (cot, masks, standard_one, standard_two, standard_mix, inverses, query, key, value, probs),
        small_params,
        (projection_output_weight, query_weight, key_weight, value_weight, second_weight, first_weight),
    )
    grads_all = across_chips(grads_all)
    wide_masks = jnp.tile(masks.T, (1, min(chips, 4)))
    latent_flat = latent.reshape(positions, embed)
    made = {}

    def sums_step(task):
        kind, of = task[:-1], task[-1]
        if task == "joint":
            return ("add", made["joint_mine"], from_sibling(made["joint_other"])), ["joint"]
        if task == "book":
            return ("add", made["book_mine"], from_sibling(made["book_other"])), ["book"]
        if task == "codes":
            return ("sum", across_chips(made["book"])), ["codebook_grad"]
        if task == "splitD":
            return ("blocks", across_chips(made["joint"])), ["keepD", "awayD"]
        if kind == "split":
            return ("split", made["mine" + of], from_sibling(made["other" + of])), ["keep" + of, "away" + of]
        if kind == "near":
            return ("add", made["keep" + of], swap_rows(made["away" + of], 1)), ["near" + of]
        if kind == "far":
            return ("add", made["near" + of], swap_rows(made["near" + of], 2)), ["far" + of]
        shape = {"A": (9, share, channels), "B": (9, share, channels), "C": (9, e_share, channels)}
        shape = shape.get(of, made["joint"].shape[1:])
        return ("join", made["far" + of], swap_rows(made["far" + of], 1), shape), ["whole" + of]

    token = vectors
    weights = {"A": (0, share), "B": (1, share), "C": (2, e_share)}
    for group in ORDER:
        task = group[0]
        if task == "post":
            *backs, small_mine, small_other, token = post_back(
                crops, row_count, width, chips, row_place, here, grad_stream, masks, quant, post_weight, vectors, decoded, token, entry_weight
            )
        elif task == "late":
            latent_late, token = late(latent_flat, token)
            latents = from_around(lambda k: latent_late)
        elif task == "attention":
            made["joint_mine"], made["joint_other"], token = attention_grads(
                dp_count, here, (normed, attended, cot, grad_q, grad_k, grad_v, small_mine, small_other), token
            )
        elif task == "scatter":
            made["book_mine"], made["book_other"], token = scatter(
                row_place, here, all_codes, latents, found, codebook.shape[0], chips, token
            )
        elif task == "assemble":
            decoded, latent_grad, token = assemble(
                crops, row_place, from_around(lambda k: backs[k]), latent, channels, token
            )
        elif task[:-1] == "weights":
            place, rows = weights[task[-1]]
            made["mine" + task[-1]], made["other" + task[-1]], token = weight_grad(
                task, width, channels, here, acts, place, rows, grads_all, wide_masks, token, part=place
            )
        else:
            steps, names = zip(*(sums_step(t) for t in group))
            *results, token = step_round("-".join(group), parity, list(steps), token)
            made.update(zip(sum(names, []), results))
    second_w, first_w, entry_w, sum_d, codebook_grad = (
        made[name] for name in ("wholeA", "wholeB", "wholeC", "wholeD", "codebook_grad")
    )

    o_w, q_w, k_w, v_w = (sum_d[i * share : (i + 1) * share] for i in range(4))
    small = sum_d[4 * share :]
    post_w = small[:e_share, :embed]
    vec = [small[i, embed : embed + share] for i in (0, 1, 2, 3, 4, 5, 8, 9, 10, 11, 12, 13)]
    post_b = small[16, embed : embed + e_share]
    gain_1, shift_1, b_entry, gain_2, shift_2, b_first, gain_m, shift_m, b_q, b_v, b_o, b_second = vec
    return (
        decoded,
        latent_grad,
        codebook_grad,
        post_w,
        post_b,
        entry_w,
        b_entry,
        gain_1,
        shift_1,
        first_w,
        b_first,
        gain_2,
        shift_2,
        second_w,
        b_second,
        gain_m,
        shift_m,
        q_w,
        b_q,
        k_w,
        v_w,
        b_v,
        o_w,
        b_o,
    )


def solution(mesh):
    def cells(depth):
        return P("dp", "row", *([None] * depth))

    return jax.shard_map(
        on_device,
        mesh=mesh,
        in_specs=(cells(2), cells(1), P("row", None)) + (P(),) * 21 + (cells(2),),
        out_specs=(
            cells(2),
            cells(2),
            P(("row", "dp"), None),
            P("dp", None),
            P("dp"),
            P(None, "dp", None),
            P("dp"),
            P("dp"),
            P("dp"),
            P(None, "dp", None),
            P("dp"),
            P("dp"),
            P("dp"),
            P(None, "dp", None),
            P("dp"),
            P("dp"),
            P("dp"),
            P("dp", None),
            P("dp"),
            P("dp", None),
            P("dp", None),
            P("dp"),
            P("dp", None),
            P("dp"),
        ),
        check_vma=False,
    )
```
